32 devices in a mesh: groups: 2 (over y), patch: 16 (over z, x, core).
Axes of the slice: x: 2, y: 2, z: 4, core: 2. Of those that a mesh axis runs over, the one named last changes fastest.
Arguments:
- node_feat: bfloat16 [8192, 512], P(('groups', 'patch')), parts along dimension 0, may hold values from -6 to 6
- local_edges: bfloat16 [24576, 512], P(('groups', 'patch')), parts along dimension 0, may hold values from -6 to 6
- far_edges: bfloat16 [8192, 512], P(('groups', 'patch')), parts along dimension 0, may hold values from -6 to 6
- local_send: int32 [24576], P(('groups', 'patch')), parts along dimension 0, may hold values from 0 to 255
- local_recv: int32 [24576], P(('groups', 'patch')), parts along dimension 0, may hold values from 0 to 255
- far_send: int32 [8192], P(('groups', 'patch')), parts along dimension 0, may hold values from 0 to 4095, as said below
- far_recv: int32 [8192], P(('groups', 'patch')), parts along dimension 0, may hold values from 0 to 4095, as said below
- edge_in: bfloat16 [2, 1536, 512], replicated, may hold values from -0.15625 to 0.15625
- edge_out: bfloat16 [2, 512, 512], replicated, may hold values from -0.25 to 0.25
- node_in: bfloat16 [2, 1024, 512], replicated, may hold values from -0.1875 to 0.1875
- node_out: bfloat16 [2, 512, 512], replicated, may hold values from -0.25 to 0.25
- edge_bias: float32 [2, 512], replicated, may hold values from -3 to 3
- edge_gain: float32 [2, 512], replicated, may hold values from 0.5 to 1.5
- edge_shift: float32 [2, 512], replicated, may hold values from -3 to 3
- node_bias: float32 [2, 512], replicated, may hold values from -3 to 3
- node_gain: float32 [2, 512], replicated, may hold values from 0.5 to 1.5
- node_shift: float32 [2, 512], replicated, may hold values from -3 to 3
Outputs:
- nodes_out: bfloat16 [8192, 512], P(('groups', 'patch')), parts along dimension 0
- local_out: bfloat16 [24576, 512], P(('groups', 'patch')), parts along dimension 0
- far_out: bfloat16 [8192, 512], P(('groups', 'patch')), parts along dimension 0
The draws below stay inside these ranges and needn't reach their ends.
There are 2 independent parts, one for each index of `groups`. The reference program is written for one: setup_inputs(seed, part) draws one part's arguments, and reference() takes and returns one part's arrays. A program takes and returns all parts, laid end to end along the dimension named above; an argument that names none is the same for every part. Nothing has to cross between parts.
Inputs may be any that keep to these rules, and one draw needn't show every extreme that they name: `far_send`: every sender lies among the first 64 nodes of its patch's block of 256. Of the 256 edges of one owner (aligned blocks of the array), at most 40 have their sender on any one patch, and exactly 40 do for some patch of every owner. `far_recv`: every receiver lies among the first 64 nodes of its patch's block of 256. Of the 256 edges of one owner (aligned blocks of the array), at most 40 have their receiver on any one patch, and exactly 40 do for some patch of every owner.
All inputs are finite; a program needn't handle non-finite values.
Results may differ from the reference program's by a relative error of at most 0.0075.
Values may be sent and summed in bfloat16 or wider, within the bound.
No kernel may reach another device: no remote copies, remote signals or barrier semaphores. Data moves between devices by JAX's collectives and lax.ppermute only.
A program may use at most 64 MiB of HBM per device.

```python
import jax
import jax.numpy as jnp
from jax import lax

D = 512
LAYERS = 2
NODE_DEV = 256
COARSE_DEV = 64
LOCAL_DEV = 768
FAR_DEV = 256
NODES = 4096
LOCAL_EDGES = 12288
FAR_EDGES = 4096
N_PATCH = 16


def far_ids(base_key):
    key_one, key_two, key_three, key_four = jax.random.split(base_key, 4)
    half = FAR_DEV // 2
    first_perm = jax.vmap(lambda sub_key: jax.random.permutation(sub_key, N_PATCH))(jax.random.split(key_one, N_PATCH))
    second_perm = jax.vmap(lambda sub_key: jax.random.permutation(sub_key, N_PATCH))(jax.random.split(key_two, N_PATCH))
    positions = jnp.arange(FAR_DEV, dtype=jnp.int32)
    first_pick = first_perm[:, positions % N_PATCH]
    second_pick = second_perm[:, (positions - half) % (N_PATCH // 4)]
    target = jnp.where(positions[None, :] < half, first_pick, second_pick)
    shuffle = jax.vmap(lambda sub_key: jax.random.permutation(sub_key, FAR_DEV))(jax.random.split(key_three, N_PATCH))
    target = jnp.take_along_axis(target, shuffle, axis=1)
    within = jax.random.randint(key_four, (N_PATCH, FAR_DEV), 0, COARSE_DEV)
    return (target * NODE_DEV + within).reshape(-1).astype(jnp.int32)


def draw_far_send(key, part):
    return far_ids(jax.random.fold_in(key, 11))


def draw_far_recv(key, part):
    return far_ids(jax.random.fold_in(key, 12))


def plant(values, own_key, smallest, largest):
    index_at = [jax.random.randint(jax.random.fold_in(own_key, axis), (), 0, length) for axis, length in enumerate(values.shape)]
    longest = values.shape.index(max(values.shape))
    neighbour = index_at[:longest] + [(index_at[longest] + 1) % values.shape[longest]] + index_at[longest + 1:]
    return values.at[tuple(index_at)].set(smallest).at[tuple(neighbour)].set(largest)


def block_scale(key, dims, cuts, smallest, largest):
    level = 1.0
    for dim, blocks in cuts:
        draws = jax.random.uniform(jax.random.fold_in(jax.random.fold_in(key, 6), dim), (blocks,), jnp.float32, smallest / len(cuts), largest / len(cuts))
        level = level * jnp.repeat(jnp.exp(draws), dims[dim] // blocks).reshape((-1,) + (1,) * (len(dims) - 1 - dim))
    return level


def normal_values(stream_key, shape, spread, reach, pieces=(), kind=jnp.bfloat16):
    result = spread * jax.random.normal(stream_key, shape, jnp.float32)
    if pieces:
        result = result * block_scale(stream_key, shape, pieces, -0.22, 0.18)
    return jnp.clip(result, -reach, reach).astype(kind)


def setup_inputs(seed: int = 0, part: int = 0) -> dict:
    streams_of = jax.random.split(jax.random.key(seed), 18)
    part_keys = jax.random.split(jax.random.fold_in(streams_of[17], part), 18)
    node_feat = normal_values(part_keys[0], (NODES, D), 1.0, 6.0, ((0, 16),))
    local_edges = normal_values(part_keys[1], (LOCAL_EDGES, D), 1.0, 6.0, ((0, 16),))
    far_edges = normal_values(part_keys[2], (FAR_EDGES, D), 1.0, 6.0, ((0, 16),))
    local_send = plant(jax.random.randint(part_keys[3], (LOCAL_EDGES,), 0, NODE_DEV), jax.random.fold_in(part_keys[3], 1), 0, NODE_DEV - 1).astype(jnp.int32)
    local_recv = plant(jax.random.randint(part_keys[4], (LOCAL_EDGES,), 0, NODE_DEV), jax.random.fold_in(part_keys[4], 1), 0, NODE_DEV - 1).astype(jnp.int32)
    far_send = draw_far_send(jax.random.fold_in(jax.random.fold_in(streams_of[17], part), 71), part)
    far_recv = draw_far_recv(jax.random.fold_in(jax.random.fold_in(streams_of[17], part), 71), part)
    edge_in = normal_values(streams_of[7], (LAYERS, 3 * D, D), (3 * D) ** -0.5, 0.15625)
    edge_out = normal_values(streams_of[8], (LAYERS, D, D), D ** -0.5, 0.25)
    node_in = normal_values(streams_of[9], (LAYERS, 2 * D, D), (2 * D) ** -0.5, 0.1875)
    node_out = normal_values(streams_of[10], (LAYERS, D, D), D ** -0.5, 0.25)
    edge_bias = normal_values(streams_of[11], (LAYERS, D), 0.5, 3.0, (), jnp.float32)
    edge_gain = jnp.clip(1.0 + 0.1 * jax.random.normal(streams_of[12], (LAYERS, D), jnp.float32), 0.5, 1.5)
    edge_shift = normal_values(streams_of[13], (LAYERS, D), 0.5, 3.0, (), jnp.float32)
    node_bias = normal_values(streams_of[14], (LAYERS, D), 0.5, 3.0, (), jnp.float32)
    node_gain = jnp.clip(1.0 + 0.1 * jax.random.normal(streams_of[15], (LAYERS, D), jnp.float32), 0.5, 1.5)
    node_shift = normal_values(streams_of[16], (LAYERS, D), 0.5, 3.0, (), jnp.float32)
    return dict(node_feat=node_feat, local_edges=local_edges, far_edges=far_edges, local_send=local_send, local_recv=local_recv, far_send=far_send, far_recv=far_recv, edge_in=edge_in, edge_out=edge_out, node_in=node_in, node_out=node_out, edge_bias=edge_bias, edge_gain=edge_gain, edge_shift=edge_shift, node_bias=node_bias, node_gain=node_gain, node_shift=node_shift)


def layer_norm(values, gain, shift):
    mean_value = lax.optimization_barrier(jnp.mean(values, axis=-1, keepdims=True))
    centred = values - mean_value
    variance = lax.optimization_barrier(jnp.mean(centred * centred, axis=-1, keepdims=True))
    return centred * jax.lax.rsqrt(variance + 1e-05) * gain + shift

def edge_update(edges, senders, receivers, w_in, w_out, bias, gain, shift):
    width = edges.shape[1]
    pre_act = jnp.dot(edges, w_in[:width], preferred_element_type=jnp.float32)
    pre_act = pre_act + jnp.dot(senders, w_in[width:2 * width], preferred_element_type=jnp.float32)
    pre_act = pre_act + jnp.dot(receivers, w_in[2 * width:], preferred_element_type=jnp.float32) + bias
    hidden = jax.nn.silu(pre_act).astype(jnp.bfloat16)
    normed = layer_norm(jnp.dot(hidden, w_out, preferred_element_type=jnp.float32), gain, shift)
    return (normed.astype(jnp.bfloat16), (edges.astype(jnp.float32) + normed).astype(jnp.bfloat16))

def node_update(nodes, summed, w_in, w_out, bias, gain, shift):
    width = nodes.shape[1]
    summed_b = summed.astype(jnp.bfloat16)
    pre_act = jnp.dot(nodes, w_in[:width], preferred_element_type=jnp.float32)
    pre_act = pre_act + jnp.dot(summed_b, w_in[width:], preferred_element_type=jnp.float32) + bias
    hidden = jax.nn.silu(pre_act).astype(jnp.bfloat16)
    normed = layer_norm(jnp.dot(hidden, w_out, preferred_element_type=jnp.float32), gain, shift)
    return (nodes.astype(jnp.float32) + normed).astype(jnp.bfloat16)

def reference(node_feat, local_edges, far_edges, local_send, local_recv, far_send, far_recv, edge_in, edge_out, node_in, node_out, edge_bias, edge_gain, edge_shift, node_bias, node_gain, node_shift):
    owner = (jnp.arange(N_PATCH * LOCAL_DEV, dtype=jnp.int32) // LOCAL_DEV).astype(jnp.int32)
    send_all = jnp.concatenate([owner * NODE_DEV + local_send, far_send]).astype(jnp.int32)
    recv_all = jnp.concatenate([owner * NODE_DEV + local_recv, far_recv]).astype(jnp.int32)
    nodes = node_feat
    edges = jnp.concatenate([local_edges, far_edges], axis=0)
    local_total = local_edges.shape[0]
    for layer_index in range(LAYERS):
        message, edges = edge_update(edges, jnp.take(nodes, send_all, axis=0), jnp.take(nodes, recv_all, axis=0), edge_in[layer_index], edge_out[layer_index], edge_bias[layer_index], edge_gain[layer_index], edge_shift[layer_index])
        summed = jax.ops.segment_sum(message.astype(jnp.float32), recv_all, num_segments=nodes.shape[0])
        nodes = node_update(nodes, summed, node_in[layer_index], node_out[layer_index], node_bias[layer_index], node_gain[layer_index], node_shift[layer_index])
    return (nodes, edges[:local_total], edges[local_total:])
```

```python
import functools

import jax
import jax.numpy as jnp
from jax import lax
from jax.experimental import pallas as pl
from jax.experimental.pallas import tpu as pltpu
from jax.sharding import PartitionSpec as P

COARSE = 64
PLANE = 4
BF = jnp.bfloat16
F32 = jnp.float32
I32 = jnp.int32


def mm(left, right):
    return jnp.dot(left, right, preferred_element_type=F32)


def silu(values):
    half = 0.5 * values
    return half * jnp.tanh(half) + half


def layer_norm(values, gain, shift):
    mean_value = jnp.mean(values, axis=-1, keepdims=True)
    centred = values - mean_value
    variance = jnp.mean(centred * centred, axis=-1, keepdims=True)
    return centred * lax.rsqrt(variance + 1e-05) * gain + shift


def match_rows(column, count, offset=0):
    where = lax.broadcasted_iota(I32, (column.shape[0], count), 1) + offset
    return jnp.where(where == column, 1.0, 0.0).astype(BF)


def match_columns(row, count, offset=0):
    where = lax.broadcasted_iota(I32, (count, row.shape[1]), 0) + offset
    return jnp.where(where == row, 1.0, 0.0).astype(BF)


def as_column(row):
    tall = jnp.broadcast_to(row.astype(F32), (8, row.shape[1]))
    return jnp.transpose(tall)[:, :1].astype(I32)


def bits(count):
    assert count & (count - 1) == 0
    return count.bit_length() - 1


def prep_kernel(node_count, lines, slot, own_ref, fs_ref, fr_ref, fe_ref, pos_ref, *slot_refs):
    own = own_ref[0]
    own_q, own_z = own & (PLANE - 1), lax.shift_right_logical(own, bits(PLANE))
    fs, fr = fs_ref[...], fr_ref[...]
    count = fs.shape[1]
    shift = bits(node_count)
    s_patch, s_within = lax.shift_right_logical(fs, shift), fs & (node_count - 1)
    r_patch, r_within = lax.shift_right_logical(fr, shift), fr & (node_count - 1)
    r_q = r_patch & (PLANE - 1)
    member = r_q ^ own_q
    s_rel = s_patch ^ (own_z * PLANE + r_q)
    s_z = lax.shift_right_logical(s_rel, bits(PLANE))
    s_block = (s_rel & (PLANE - 1)) * lines + (s_z ^ lax.shift_right_logical(s_z, 1))
    r_z = lax.shift_right_logical(r_patch, bits(PLANE)) ^ own_z
    r_block = (r_z ^ lax.shift_right_logical(r_z, 1)) + 1
    flags = jnp.where(lax.broadcasted_iota(I32, (8, count), 0) == member, 1.0, 0.0)
    before = jnp.where(
        lax.broadcasted_iota(I32, (count, count), 0) < lax.broadcasted_iota(I32, (count, count), 1),
        1.0,
        0.0,
    ).astype(BF)
    rank = jnp.sum(flags * mm(flags.astype(BF), before), axis=0, keepdims=True)
    pos = member * slot + rank.astype(I32)
    pos_ref[...] = pos
    row_at = lax.broadcasted_iota(I32, (8, count), 0)
    meta = jnp.where(row_at == 0, s_block, 0)
    meta = jnp.where(row_at == 1, s_within, meta)
    meta = jnp.where(row_at == 2, r_block, meta)
    meta = jnp.where(row_at == 3, r_within, meta).astype(F32).astype(BF)
    for m, ref in enumerate(slot_refs):
        moved = match_columns(pos - m * slot, slot)
        ref[0:slot, :] = mm(moved, fe_ref[...]).astype(BF)
        tail = lax.dot_general(meta, moved, (((1,), (1,)), ((), ())), preferred_element_type=F32)
        ref[slot:, :] = jnp.zeros((ref.shape[0] - slot, ref.shape[1]), BF)
        ref[slot : slot + 16, 0:slot] = jnp.concatenate(
            [tail, jnp.zeros((8, slot), F32)], axis=0
        ).astype(BF)


def edge_mlp(edges, senders, receivers, w_in, w_out, vec_ref):
    stacked = jnp.concatenate([edges, senders, receivers], axis=1)
    hidden = silu(mm(stacked, w_in) + vec_ref[0:1, :]).astype(BF)
    return layer_norm(mm(hidden, w_out), vec_ref[1:2, :], vec_ref[2:3, :])


def local_kernel(
    block, nodes_ref, edges_ref, send_ref, recv_ref, win_ref, wout_ref, vec_ref, new_ref, sum_ref
):
    node_count = nodes_ref.shape[0]
    nodes = nodes_ref[...]
    for i in range(edges_ref.shape[0] // block):
        rows = slice(i * block, (i + 1) * block)
        send, recv = send_ref[:, rows], recv_ref[:, rows]
        edges = edges_ref[rows, :]
        normed = edge_mlp(
            edges,
            mm(match_rows(as_column(send), node_count), nodes).astype(BF),
            mm(match_rows(as_column(recv), node_count), nodes).astype(BF),
            win_ref[...],
            wout_ref[...],
            vec_ref,
        )
        new_ref[rows, :] = (edges.astype(F32) + normed).astype(BF)
        part = mm(match_columns(recv, node_count), normed.astype(BF))
        if i == 0:
            sum_ref[...] = part
        else:
            sum_ref[...] += part


def far_kernel(lines, slot, *refs):
    slots, tables = refs[0:PLANE], refs[PLANE : 2 * PLANE]
    win_ref, wout_ref, vec_ref = refs[2 * PLANE : 2 * PLANE + 3]
    outs = refs[2 * PLANE + 3 :]
    new_refs, own_ref, part_refs = outs[0:PLANE], outs[PLANE], outs[PLANE + 1 :]
    span = lines * COARSE
    total = None
    for pair in range(0, PLANE, 2):
        columns_s, columns_r, rows_r = [], [], []
        for ref in slots[pair : pair + 2]:
            meta = ref[slot : slot + 16, :].astype(F32)[0:8, 0 : -(-slot // 128) * 128]
            tall = jnp.transpose(meta)[0:slot, :]
            columns_s.append((tall[:, 0:1] * COARSE + tall[:, 1:2]).astype(I32))
            columns_r.append((tall[:, 2:3] * COARSE + tall[:, 3:4]).astype(I32) - COARSE)
            rows_r.append((meta[2:3, 0:slot] * COARSE + meta[3:4, 0:slot]).astype(I32) - COARSE)
        column_s, column_r = jnp.concatenate(columns_s, axis=0), jnp.concatenate(columns_r, axis=0)
        senders = None
        for q, table in enumerate(tables):
            piece = mm(match_rows(column_s, span, q * span), table[...])
            senders = piece if senders is None else senders + piece
        receivers = mm(match_rows(column_r, span), tables[0][...])
        edges = jnp.concatenate([ref[0:slot, :] for ref in slots[pair : pair + 2]], axis=0)
        normed = edge_mlp(
            edges, senders.astype(BF), receivers.astype(BF), win_ref[...], wout_ref[...], vec_ref
        )
        new = (edges.astype(F32) + normed).astype(BF)
        message = normed.astype(BF)
        for i in range(2):
            new_refs[pair + i][0:slot, :] = new[i * slot : (i + 1) * slot, :]
            new_refs[pair + i][slot:, :] = slots[pair + i][slot:, :]
            part = mm(match_columns(rows_r[i], span), message[i * slot : (i + 1) * slot, :])
            total = part if total is None else total + part
    own_ref[...] = total[0:COARSE, :]
    for i, ref in enumerate(part_refs):
        ref[...] = total[(i + 1) * COARSE : (i + 2) * COARSE, :].astype(BF)


def node_kernel(nodes_ref, sum_ref, own_ref, *refs):
    part_refs, (win_ref, wout_ref, vec_ref), outs = refs[:-5], refs[-5:-2], refs[-2:]
    far = own_ref[...]
    for ref in part_refs:
        far = far + ref[...].astype(F32)
    sums = jnp.concatenate([sum_ref[0:COARSE, :] + far, sum_ref[COARSE:, :]], axis=0).astype(BF)
    nodes = nodes_ref[...]
    stacked = jnp.concatenate([nodes, sums], axis=1)
    hidden = silu(mm(stacked, win_ref[...]) + vec_ref[0:1, :]).astype(BF)
    normed = layer_norm(mm(hidden, wout_ref[...]), vec_ref[1:2, :], vec_ref[2:3, :])
    new = (nodes.astype(F32) + normed).astype(BF)
    outs[0][...] = new
    outs[1][...] = new[0:COARSE, :]


def restore_kernel(slot, pos_ref, *refs):
    slots, out_ref = refs[:-1], refs[-1]
    column = as_column(pos_ref[...])
    total = None
    for m, ref in enumerate(slots):
        piece = mm(match_rows(column - m * slot, slot), ref[0:slot, :])
        total = piece if total is None else total + piece
    out_ref[...] = total.astype(BF)


def call(kernel, outs, args, flops, limit, scalars=0):
    bytes_accessed = sum(a.size * a.dtype.itemsize for a in args)
    bytes_accessed += sum(o.size * o.dtype.itemsize for o in outs)
    specs = [pl.BlockSpec(memory_space=pltpu.SMEM)] * scalars
    specs += [pl.BlockSpec(memory_space=pltpu.VMEM)] * (len(args) - scalars)
    return pl.pallas_call(
        kernel,
        out_shape=outs,
        in_specs=specs,
        out_specs=[pl.BlockSpec(memory_space=pltpu.VMEM)] * len(outs),
        compiler_params=pltpu.CompilerParams(vmem_limit_bytes=limit),
        cost_estimate=pl.CostEstimate(flops=flops, bytes_accessed=bytes_accessed, transcendentals=0),
    )(*args)


def body(
    node_feat,
    local_edges,
    far_edges,
    local_send,
    local_recv,
    far_send,
    far_recv,
    edge_in,
    edge_out,
    node_in,
    node_out,
    edge_bias,
    edge_gain,
    edge_shift,
    node_bias,
    node_gain,
    node_shift,
):
    devices = lax.axis_size("patch")
    lines = devices // PLANE
    node_count, width = node_feat.shape
    far_count, local_count = far_edges.shape[0], local_edges.shape[0]
    slot = lines * (5 * far_count // (2 * devices))
    padded = -(-(slot + 4) // 16) * 16
    layers = edge_in.shape[0]
    limit = (24 if lines <= 4 else 56) * 2**20
    shape = jax.ShapeDtypeStruct
    place = [0] * lines
    for z in range(lines):
        place[z ^ (z >> 1)] = z

    def swap(values, distance):
        return lax.ppermute(values, "patch", [(i, i ^ distance) for i in range(devices)])

    def gather(own):
        if lines == 4:
            z3, z1 = swap(own, 12), swap(own, 4)
            z2 = swap(z3, 4)
            first = jnp.concatenate([own, z1, z3], axis=0)
            table = jnp.concatenate([first, z2], axis=0)
            across = jnp.concatenate([swap(first, 2), swap(z2, 2)], axis=0)
        else:
            table = jnp.concatenate(
                [own if z == 0 else swap(own, PLANE * z) for z in place], axis=0
            )
            across = swap(table, 2)
        return (table, swap(table, 1), across, swap(across, 1))

    own = lax.axis_index("patch").reshape(1).astype(I32)
    fs, fr = far_send.reshape(1, -1), far_recv.reshape(1, -1)
    ls, lr = local_send.reshape(1, -1), local_recv.reshape(1, -1)
    prepared = call(
        functools.partial(prep_kernel, node_count, lines, slot),
        [shape((1, far_count), I32)] + [shape((padded, width), BF)] * PLANE,
        [own, fs, fr, far_edges],
        2 * PLANE * slot * far_count * width,
        limit,
        scalars=1,
    )
    pos, slots = prepared[0], prepared[1:]
    slots = [slots[0]] + [swap(slots[m], m) for m in range(1, PLANE)]
    nodes, coarse, local = node_feat, node_feat[:COARSE], local_edges
    for l in range(layers):
        edge_vec = jnp.stack([edge_bias[l], edge_gain[l], edge_shift[l]])
        node_vec = jnp.stack([node_bias[l], node_gain[l], node_shift[l]])
        tables = gather(coarse)
        far_rows = PLANE * slot
        far = call(
            functools.partial(far_kernel, lines, slot),
            [shape((padded, width), BF)] * PLANE
            + [shape((COARSE, width), F32)]
            + [shape((COARSE, width), BF)] * (lines - 1),
            [*slots, *tables, edge_in[l], edge_out[l], edge_vec],
            2 * far_rows * width * (6 * lines * COARSE + 4 * width),
            limit,
        )
        slots = far[:PLANE]
        parts = [swap(v, PLANE * place[i + 1]) for i, v in enumerate(far[PLANE + 1 :])]
        local, sums = call(
            functools.partial(local_kernel, min(local_count, 256)),
            [shape((local_count, width), BF), shape((node_count, width), F32)],
            [nodes, local, ls, lr, edge_in[l], edge_out[l], edge_vec],
            2 * local_count * width * (3 * node_count + 4 * width),
            limit,
        )
        nodes, coarse = call(
            node_kernel,
            [shape((node_count, width), BF), shape((COARSE, width), BF)],
            [nodes, sums, far[PLANE], *parts, node_in[l], node_out[l], node_vec],
            2 * node_count * width * 3 * width,
            limit,
        )
    slots = [slots[0]] + [swap(slots[m], m) for m in range(1, PLANE)]
    far_out = call(
        functools.partial(restore_kernel, slot),
        [shape((far_count, width), BF)],
        [pos, *slots],
        2 * PLANE * slot * far_count * width,
        limit,
    )[0]
    return (nodes, local, far_out)


def solution(mesh):
    split = P(("groups", "patch"), None)
    line = P(("groups", "patch"))
    return jax.shard_map(
        body,
        mesh=mesh,
        in_specs=(split,) * 3 + (line,) * 4 + (P(),) * 10,
        out_specs=(split,) * 3,
        check_vma=False,
    )
```

```python
import functools

import jax
import jax.numpy as jnp
from jax import lax
from jax.experimental import pallas as pl
from jax.experimental.pallas import tpu as pltpu
from jax.sharding import PartitionSpec as P

COARSE = 64
PLANE = 4
BF = jnp.bfloat16
F32 = jnp.float32
I32 = jnp.int32


def mm(left, right):
    return jnp.dot(left, right, preferred_element_type=F32)


def silu(values):
    half = 0.5 * values
    return half * jnp.tanh(half) + half


def layer_norm(values, gain, shift):
    mean_value = jnp.mean(values, axis=-1, keepdims=True)
    centred = values - mean_value
    variance = jnp.mean(centred * centred, axis=-1, keepdims=True)
    return centred * lax.rsqrt(variance + 1e-05) * gain + shift


def match_rows(column, count, offset=0):
    where = lax.broadcasted_iota(I32, (column.shape[0], count), 1) + offset
    return jnp.where(where == column, 1.0, 0.0).astype(BF)


def match_columns(row, count, offset=0):
    where = lax.broadcasted_iota(I32, (count, row.shape[1]), 0) + offset
    return jnp.where(where == row, 1.0, 0.0).astype(BF)


def as_column(row):
    tall = jnp.broadcast_to(row.astype(F32), (8, row.shape[1]))
    return jnp.transpose(tall)[:, :1].astype(I32)


def bits(count):
    assert count & (count - 1) == 0
    return count.bit_length() - 1


def prep_kernel(node_count, lines, slot, own_ref, fs_hbm, fr_hbm, fe_hbm, nodes_hbm, *refs):
    pos_ref, coarse_ref, rest_ref, slot_refs = *refs[0:3], refs[3 : 3 + PLANE]
    fs_ref, fr_ref, fe_ref, sems = refs[3 + PLANE :]
    moves = [
        (fs_hbm, fs_ref),
        (fr_hbm, fr_ref),
        (fe_hbm, fe_ref),
        (nodes_hbm.at[0:COARSE, :], coarse_ref),
        (nodes_hbm.at[COARSE:, :], rest_ref),
    ]
    copies = [pltpu.make_async_copy(a, b, sems.at[i]) for i, (a, b) in enumerate(moves)]
    for copy in copies:
        copy.start()
    for copy in copies[0:3]:
        copy.wait()
    own = own_ref[0]
    own_q, own_z = own & (PLANE - 1), lax.shift_right_logical(own, bits(PLANE))
    fs, fr = fs_ref[...], fr_ref[...]
    count = fs.shape[1]
    shift = bits(node_count)
    s_patch, s_within = lax.shift_right_logical(fs, shift), fs & (node_count - 1)
    r_patch, r_within = lax.shift_right_logical(fr, shift), fr & (node_count - 1)
    r_q = r_patch & (PLANE - 1)
    member = r_q ^ own_q
    s_rel = s_patch ^ (own_z * PLANE + r_q)
    s_z = lax.shift_right_logical(s_rel, bits(PLANE))
    s_block = (s_rel & (PLANE - 1)) * lines + (s_z ^ lax.shift_right_logical(s_z, 1))
    r_z = lax.shift_right_logical(r_patch, bits(PLANE)) ^ own_z
    r_block = (r_z ^ lax.shift_right_logical(r_z, 1)) + 1
    flags = jnp.where(lax.broadcasted_iota(I32, (8, count), 0) == member, 1.0, 0.0)
    before = jnp.where(
        lax.broadcasted_iota(I32, (count, count), 0) < lax.broadcasted_iota(I32, (count, count), 1),
        1.0,
        0.0,
    ).astype(BF)
    rank = jnp.sum(flags * mm(flags.astype(BF), before), axis=0, keepdims=True)
    pos = member * slot + rank.astype(I32)
    pos_ref[...] = pos
    row_at = lax.broadcasted_iota(I32, (8, count), 0)
    meta = jnp.where(row_at == 0, s_block, 0)
    meta = jnp.where(row_at == 1, s_within, meta)
    meta = jnp.where(row_at == 2, r_block, meta)
    meta = jnp.where(row_at == 3, r_within, meta).astype(F32).astype(BF)
    for m, ref in enumerate(slot_refs):
        moved = match_columns(pos - m * slot, slot)
        ref[0:slot, :] = mm(moved, fe_ref[...]).astype(BF)
        tail = lax.dot_general(meta, moved, (((1,), (1,)), ((), ())), preferred_element_type=F32)
        ref[slot:, :] = jnp.zeros((ref.shape[0] - slot, ref.shape[1]), BF)
        ref[slot : slot + 16, 0:slot] = jnp.concatenate(
            [tail, jnp.zeros((8, slot), F32)], axis=0
        ).astype(BF)
    for copy in copies[3:]:
        copy.wait()


def load_kernel(*refs):
    count = len(refs) // 2
    sources, held, sems = refs[:count], refs[count : 2 * count], refs[-1]
    copies = [pltpu.make_async_copy(a, b, sems.at[i]) for i, (a, b) in enumerate(zip(sources, held))]
    for copy in copies:
        copy.start()
    for copy in copies:
        copy.wait()


def edge_tail(pre_act, w_out, bias, gain, shift):
    hidden = silu(pre_act + bias).astype(BF)
    return layer_norm(mm(hidden, w_out), gain, shift)


def local_kernel(layer, rows, *refs):
    coarse_ref, rest_ref, edges_ref, send_ref, recv_ref, win_ref, wout_ref = refs[0:7]
    vec_refs, before, (new_ref, sum_ref) = refs[7:10], refs[10:-2], refs[-2:]
    nodes = jnp.concatenate([coarse_ref[...], rest_ref[...]], axis=0)
    node_count = nodes.shape[0]
    if before:
        new_ref[0 : rows.start, :] = before[0][0 : rows.start, :]
    total = before[1][...] if before else None
    block = min(rows.stop - rows.start, 256)
    for start in range(rows.start, rows.stop, block):
        send = send_ref[start : start + block].reshape(1, -1)
        recv = recv_ref[start : start + block].reshape(1, -1)
        edges = edges_ref[start : start + block, :]
        senders = mm(match_rows(as_column(send), node_count), nodes).astype(BF)
        receivers = mm(match_rows(as_column(recv), node_count), nodes).astype(BF)
        stacked = jnp.concatenate([edges, senders, receivers], axis=1)
        normed = edge_tail(
            mm(stacked, win_ref[layer]), wout_ref[layer], *[v[layer : layer + 1, :] for v in vec_refs]
        )
        new_ref[start : start + block, :] = (edges.astype(F32) + normed).astype(BF)
        part = mm(match_columns(recv, node_count), normed.astype(BF))
        total = part if total is None else total + part
    sum_ref[...] = total


def slot_indices(ref, slot):
    meta = ref[slot : slot + 16, :].astype(F32)[0:8, 0 : -(-slot // 128) * 128]
    tall = jnp.transpose(meta)[0:slot, :]
    send_column = (tall[:, 0:1] * COARSE + tall[:, 1:2]).astype(I32)
    recv_column = (tall[:, 2:3] * COARSE + tall[:, 3:4]).astype(I32) - COARSE
    recv_row = (meta[2:3, 0:slot] * COARSE + meta[3:4, 0:slot]).astype(I32) - COARSE
    return send_column, recv_column, recv_row


def far_first_kernel(layer, lines, slot, *refs):
    slots, tables, win_ref, out_ref = refs[0:PLANE], refs[PLANE : PLANE + 2], refs[-2], refs[-1]
    span = lines * COARSE
    for pair in range(0, PLANE, 2):
        found = [slot_indices(ref, slot) for ref in slots[pair : pair + 2]]
        column_s = jnp.concatenate([f[0] for f in found], axis=0)
        column_r = jnp.concatenate([f[1] for f in found], axis=0)
        senders = mm(match_rows(column_s, span), tables[0][...])
        senders = senders + mm(match_rows(column_s, span, span), tables[1][...])
        receivers = mm(match_rows(column_r, span), tables[0][...])
        edges = jnp.concatenate([ref[0:slot, :] for ref in slots[pair : pair + 2]], axis=0)
        stacked = jnp.concatenate([edges, senders.astype(BF), receivers.astype(BF)], axis=1)
        out_ref[pair * slot : (pair + 2) * slot, :] = mm(stacked, win_ref[layer])


def far_second_kernel(layer, lines, slot, pairs, keep, chained, *refs):
    count = 2 * len(pairs)
    slots, tables, refs = refs[0:count], refs[count : count + 2], refs[count + 2 :]
    pre_ref, sum_ref, win_ref, wout_ref, refs = *refs[0:4], refs[4:]
    vecs, refs = [v[layer : layer + 1, :] for v in refs[0:3]], refs[3:]
    new_refs, outs = refs[0:count], refs[count:]
    span, width = lines * COARSE, pre_ref.shape[1]
    total = None
    for i, pair in enumerate(pairs):
        own = slots[2 * i : 2 * i + 2]
        found = [slot_indices(ref, slot) for ref in own]
        column_s = jnp.concatenate([f[0] for f in found], axis=0)
        senders = mm(match_rows(column_s, span, 2 * span), tables[0][...])
        senders = senders + mm(match_rows(column_s, span, 3 * span), tables[1][...])
        pre_act = pre_ref[pair * slot : (pair + 2) * slot, :]
        pre_act = pre_act + mm(senders.astype(BF), win_ref[layer, width : 2 * width, :])
        normed = edge_tail(pre_act, wout_ref[layer], *vecs)
        edges = jnp.concatenate([ref[0:slot, :] for ref in own], axis=0)
        new = (edges.astype(F32) + normed).astype(BF)
        message = normed.astype(BF)
        for j in range(2):
            new_refs[2 * i + j][0:slot, :] = new[j * slot : (j + 1) * slot, :]
            if keep:
                new_refs[2 * i + j][slot:, :] = own[j][slot:, :]
            part = mm(match_columns(found[j][2], span), message[j * slot : (j + 1) * slot, :])
            total = part if total is None else total + part
    if len(outs) == 1:
        outs[0][...] = total
        outs[0][0:COARSE, :] += sum_ref[0:COARSE, :]
        return
    if chained:
        total = total + sum_ref[...]
        outs[0][...] = total[0:COARSE, :]
    else:
        outs[0][...] = total[0:COARSE, :] + sum_ref[0:COARSE, :]
    for i, ref in enumerate(outs[1:]):
        ref[...] = total[(i + 1) * COARSE : (i + 2) * COARSE, :].astype(BF)


def node_update(layer, nodes, sums, win_ref, wout_ref, vec_refs):
    stacked = jnp.concatenate([nodes, sums.astype(BF)], axis=1)
    bias, gain, shift = [v[layer : layer + 1, :] for v in vec_refs]
    normed = edge_tail(mm(stacked, win_ref[layer]), wout_ref[layer], bias, gain, shift)
    return (nodes.astype(F32) + normed).astype(BF)


def rest_kernel(layer, nodes_ref, sum_ref, win_ref, wout_ref, *refs):
    sums = sum_ref[COARSE:, :]
    refs[-1][...] = node_update(layer, nodes_ref[...], sums, win_ref, wout_ref, refs[0:3])


def coarse_kernel(layer, nodes_ref, rest_ref, own_ref, *refs):
    part_refs, (win_ref, wout_ref), vec_refs, out_ref = refs[:-6], refs[-6:-4], refs[-4:-1], refs[-1]
    sums = own_ref[...]
    for ref in part_refs:
        sums = sums + ref[...].astype(F32)
    out_ref[0:COARSE, :] = node_update(layer, nodes_ref[...], sums, win_ref, wout_ref, vec_refs)
    if out_ref.shape[0] > COARSE:
        out_ref[COARSE:, :] = rest_ref[...]


def restore_kernel(slot, pos_ref, *refs):
    slots, out_ref = refs[:-1], refs[-1]
    column = as_column(pos_ref[...])
    total = None
    for m, ref in enumerate(slots):
        piece = mm(match_rows(column - m * slot, slot), ref[0:slot, :])
        total = piece if total is None else total + piece
    out_ref[...] = total.astype(BF)


def call(kernel, outs, args, flops, limit, first=None, scratch=()):
    bytes_accessed = sum(a.size * a.dtype.itemsize for a in args)
    bytes_accessed += sum(o.size * o.dtype.itemsize for o in outs)
    whole = pl.BlockSpec(memory_space=pltpu.VMEM)
    specs = [whole] * len(args)
    if first is not None:
        specs = [pl.BlockSpec(memory_space=pltpu.SMEM)] * first
        specs += [pl.BlockSpec(memory_space=pltpu.HBM)] * (len(args) - first)
        args = list(args[:first]) + [
            pltpu.with_memory_space_constraint(a, pltpu.HBM) for a in args[first:]
        ]
    return pl.pallas_call(
        kernel,
        out_shape=outs,
        in_specs=specs,
        out_specs=[whole] * len(outs),
        scratch_shapes=scratch,
        compiler_params=pltpu.CompilerParams(vmem_limit_bytes=limit),
        cost_estimate=pl.CostEstimate(flops=flops, bytes_accessed=bytes_accessed, transcendentals=0),
    )(*args)


def body(
    node_feat,
    local_edges,
    far_edges,
    local_send,
    local_recv,
    far_send,
    far_recv,
    edge_in,
    edge_out,
    node_in,
    node_out,
    edge_bias,
    edge_gain,
    edge_shift,
    node_bias,
    node_gain,
    node_shift,
):
    devices = lax.axis_size("patch")
    lines = devices // PLANE
    node_count, width = node_feat.shape
    far_count, local_count = far_edges.shape[0], local_edges.shape[0]
    slot = lines * (5 * far_count // (2 * devices))
    padded = -(-(slot + 4) // 16) * 16
    layers = edge_in.shape[0]
    limit = (24 if lines <= 4 else 56) * 2**20
    shape = jax.ShapeDtypeStruct
    place = [0] * lines
    for z in range(lines):
        place[z ^ (z >> 1)] = z

    def swap(values, distance):
        return lax.ppermute(values, "patch", [(i, i ^ distance) for i in range(devices)])

    own = lax.axis_index("patch").reshape(1).astype(I32)
    fs, fr = far_send.reshape(1, -1), far_recv.reshape(1, -1)
    tied = lax.optimization_barrier
    prepared = call(
        functools.partial(prep_kernel, node_count, lines, slot),
        [shape((1, far_count), I32), shape((COARSE, width), BF)]
        + [shape((node_count - COARSE, width), BF)]
        + [shape((padded, width), BF)] * PLANE,
        [own, fs, fr, far_edges, node_feat],
        2 * PLANE * slot * far_count * width,
        limit,
        first=1,
        scratch=[
            pltpu.VMEM((1, far_count), I32),
            pltpu.VMEM((1, far_count), I32),
            pltpu.VMEM((far_count, width), BF),
            pltpu.SemaphoreType.DMA((5,)),
        ],
    )
    pos, coarse, rest, slots = *prepared[0:3], prepared[3:]
    slots = [slots[0]] + [swap(slots[m], m) for m in range(1, PLANE)]
    fetched = [local_edges, local_send, local_recv, edge_in, edge_out, node_in, node_out]
    fetched += [edge_bias, edge_gain, edge_shift, node_bias, node_gain, node_shift]
    fetched = call(
        load_kernel,
        [shape(v.shape, v.dtype) for v in fetched],
        fetched,
        0,
        limit,
        first=0,
        scratch=[pltpu.SemaphoreType.DMA((len(fetched),))],
    )
    far_rows, span = PLANE * slot, lines * COARSE
    hop = None
    if lines == 4:
        hop = [swap(coarse, 12), swap(coarse, 4)]
        *hop, fetched, slots = tied((*hop, fetched, slots))
    local, local_send, local_recv, edge_in, edge_out, node_in, node_out = fetched[0:7]
    edge_vecs, node_vecs = fetched[7:10], fetched[10:13]
    for l in range(layers):
        last = l == layers - 1
        cut = local_count // 3 * 2 // 256 * 256
        pieces = [slice(0, cut), slice(cut, local_count)] if cut else [slice(0, local_count)]

        def local_part(rows, before=()):
            return call(
                functools.partial(local_kernel, l, rows),
                [shape((rows.stop, width), BF), shape((node_count, width), F32)],
                [coarse, rest, local, local_send, local_recv, edge_in, edge_out, *edge_vecs, *before],
                2 * (rows.stop - rows.start) * width * (3 * node_count + 4 * width),
                limit,
            )

        done = local_part(pieces[0])
        if lines == 4:
            z3, z1 = hop if l == 0 else (swap(coarse, 12), swap(coarse, 4))
            if l:
                z3, z1, done = tied((z3, z1, done))
            near = jnp.concatenate([coarse, z1, z3], axis=0)
            z2, near_across = swap(z3, 4), swap(near, 2)
            for rows in pieces[1:]:
                done = local_part(rows, done)
            z2, done = tied((z2, done))
            table = jnp.concatenate([near, z2], axis=0)
            across = [near_across, swap(z2, 2)]
        else:
            table = [coarse if z == 0 else swap(coarse, PLANE * z) for z in place]
            table = jnp.concatenate(table, axis=0)
            across = [swap(table, 2)]
            for rows in pieces[1:]:
                done = local_part(rows, done)
        local, sums = done
        tables = [table, swap(table, 1)]
        pre_act = call(
            functools.partial(far_first_kernel, l, lines, slot),
            [shape((far_rows, width), F32)],
            [*slots, *tables, edge_in],
            2 * far_rows * width * (3 * span + 3 * width),
            limit,
        )[0]
        across[-1], pre_act = tied((across[-1], pre_act))
        across = jnp.concatenate(across, axis=0)
        tables += [across, swap(across, 1)]
        kept = [shape((slot if last else padded, width), BF)]
        parts_shape = [shape((COARSE, width), F32)] + [shape((COARSE, width), BF)] * (lines - 1)
        ends = [pre_act, sums, edge_in, edge_out, *edge_vecs]
        work = 2 * far_rows * width * (3 * span + 2 * width)
        if last:
            far = call(
                functools.partial(far_second_kernel, l, lines, slot, (2,), False, False),
                kept * 2 + [shape((span, width), F32)],
                [*slots[2:], *tables[2:], *ends],
                work // 2,
                limit,
            )
            ends[1] = far[2]
            more = call(
                functools.partial(far_second_kernel, l, lines, slot, (0,), False, True),
                kept * 2 + parts_shape,
                [*slots[:2], *tables[2:], *ends],
                work // 2,
                limit,
            )
            slots, parts = [*more[:2], *far[:2]], more[2:]
        else:
            far = call(
                functools.partial(far_second_kernel, l, lines, slot, (0, 2), True, False),
                kept * 4 + parts_shape,
                [*slots, *tables[2:], *ends],
                work,
                limit,
            )
            slots, parts = [*far[:PLANE]], far[PLANE:]
        far_parts = [swap(parts[i], PLANE * place[i]) for i in range(lines - 1, 0, -1)]
        parts = [parts[0]] + far_parts[::-1]
        ends = [node_in, node_out, *node_vecs]
        rest = call(
            functools.partial(rest_kernel, l),
            [shape((node_count - COARSE, width), BF)],
            [rest, sums, *ends],
            6 * (node_count - COARSE) * width * width,
            limit,
        )[0]
        coarse = call(
            functools.partial(coarse_kernel, l),
            [shape((node_count if last else COARSE, width), BF)],
            [coarse, rest, *parts, *ends],
            6 * COARSE * width * width,
            limit,
        )[0]
    slots = [slots[0]] + [swap(slots[m], m) for m in range(1, PLANE)]
    far_out = call(
        functools.partial(restore_kernel, slot),
        [shape((far_count, width), BF)],
        [pos, *slots],
        2 * PLANE * slot * far_count * width,
        limit,
    )[0]
    return (coarse, local, far_out)


def solution(mesh):
    split = P(("groups", "patch"), None)
    line = P(("groups", "patch"))
    return jax.shard_map(
        body,
        mesh=mesh,
        in_specs=(split,) * 3 + (line,) * 4 + (P(),) * 10,
        out_specs=(split,) * 3,
        check_vma=False,
    )
```

```python
import functools

import jax
import jax.numpy as jnp
from jax import lax
from jax.experimental import pallas as pl
from jax.experimental.pallas import tpu as pltpu
from jax.sharding import PartitionSpec as P

COARSE = 64
PLANE = 4
BF = jnp.bfloat16
F32 = jnp.float32
I32 = jnp.int32


def mm(left, right):
    return jnp.dot(left, right, preferred_element_type=F32)


def silu(values):
    half = 0.5 * values
    return half * jnp.tanh(half) + half


def layer_norm(values, gain, shift):
    mean_value = jnp.mean(values, axis=-1, keepdims=True)
    centred = values - mean_value
    variance = jnp.mean(centred * centred, axis=-1, keepdims=True)
    return centred * lax.rsqrt(variance + 1e-05) * gain + shift


def match_rows(column, count, offset=0):
    where = lax.broadcasted_iota(I32, (column.shape[0], count), 1) + offset
    return jnp.where(where == column, 1.0, 0.0).astype(BF)


def match_columns(row, count, offset=0):
    where = lax.broadcasted_iota(I32, (count, row.shape[1]), 0) + offset
    return jnp.where(where == row, 1.0, 0.0).astype(BF)


def as_column(row):
    tall = jnp.broadcast_to(row.astype(F32), (8, row.shape[1]))
    return jnp.transpose(tall)[:, :1].astype(I32)


def bits(count):
    assert count & (count - 1) == 0
    return count.bit_length() - 1


def prep_kernel(node_count, lines, slot, own_ref, fs_hbm, fr_hbm, fe_hbm, nodes_hbm, *refs):
    pos_ref, coarse_ref, rest_ref, slot_refs = *refs[0:3], refs[3 : 3 + PLANE]
    fs_ref, fr_ref, fe_ref, sems = refs[3 + PLANE :]
    moves = [
        (fs_hbm, fs_ref),
        (fr_hbm, fr_ref),
        (fe_hbm, fe_ref),
        (nodes_hbm.at[0:COARSE, :], coarse_ref),
        (nodes_hbm.at[COARSE:, :], rest_ref),
    ]
    copies = [pltpu.make_async_copy(a, b, sems.at[i]) for i, (a, b) in enumerate(moves)]
    for copy in copies:
        copy.start()
    for copy in copies[0:3]:
        copy.wait()
    own = own_ref[0]
    own_q, own_z = own & (PLANE - 1), lax.shift_right_logical(own, bits(PLANE))
    fs, fr = fs_ref[...], fr_ref[...]
    count = fs.shape[1]
    shift = bits(node_count)
    s_patch, s_within = lax.shift_right_logical(fs, shift), fs & (node_count - 1)
    r_patch, r_within = lax.shift_right_logical(fr, shift), fr & (node_count - 1)
    r_q = r_patch & (PLANE - 1)
    member = r_q ^ own_q
    s_rel = s_patch ^ (own_z * PLANE + r_q)
    s_z = lax.shift_right_logical(s_rel, bits(PLANE))
    s_block = (s_rel & (PLANE - 1)) * lines + (s_z ^ lax.shift_right_logical(s_z, 1))
    r_z = lax.shift_right_logical(r_patch, bits(PLANE)) ^ own_z
    r_block = (r_z ^ lax.shift_right_logical(r_z, 1)) + 1
    flags = jnp.where(lax.broadcasted_iota(I32, (8, count), 0) == member, 1.0, 0.0)
    before = jnp.where(
        lax.broadcasted_iota(I32, (count, count), 0) < lax.broadcasted_iota(I32, (count, count), 1),
        1.0,
        0.0,
    ).astype(BF)
    rank = jnp.sum(flags * mm(flags.astype(BF), before), axis=0, keepdims=True)
    pos = member * slot + rank.astype(I32)
    pos_ref[...] = pos
    row_at = lax.broadcasted_iota(I32, (8, count), 0)
    meta = jnp.where(row_at == 0, s_block, 0)
    meta = jnp.where(row_at == 1, s_within, meta)
    meta = jnp.where(row_at == 2, r_block, meta)
    meta = jnp.where(row_at == 3, r_within, meta).astype(F32).astype(BF)
    for m, ref in enumerate(slot_refs):
        moved = match_columns(pos - m * slot, slot)
        ref[0:slot, :] = mm(moved, fe_ref[...]).astype(BF)
        tail = lax.dot_general(meta, moved, (((1,), (1,)), ((), ())), preferred_element_type=F32)
        ref[slot:, :] = jnp.zeros((ref.shape[0] - slot, ref.shape[1]), BF)
        ref[slot : slot + 16, 0:slot] = jnp.concatenate(
            [tail, jnp.zeros((8, slot), F32)], axis=0
        ).astype(BF)
    for copy in copies[3:]:
        copy.wait()


def load_kernel(picks, *refs):
    sources, held, sems = refs[: -len(picks) - 1], refs[-len(picks) - 1 : -1], refs[-1]
    copies = []
    for i, (which, layer) in enumerate(picks):
        source = sources[which] if layer is None else sources[which].at[layer]
        copies.append(pltpu.make_async_copy(source, held[i], sems.at[i]))
        copies[i].start()
    for copy in copies:
        copy.wait()


def edge_tail(pre_act, w_out, bias, gain, shift):
    hidden = silu(pre_act + bias).astype(BF)
    return layer_norm(mm(hidden, w_out), gain, shift)


def local_kernel(layer, rows, *refs):
    coarse_ref, rest_ref, edges_ref, send_ref, recv_ref, win_ref, wout_ref = refs[0:7]
    vec_refs, before, (new_ref, sum_ref) = refs[7:10], refs[10:-2], refs[-2:]
    nodes = jnp.concatenate([coarse_ref[...], rest_ref[...]], axis=0)
    node_count = nodes.shape[0]
    if before:
        new_ref[0 : rows.start, :] = before[0][0 : rows.start, :]
    total = before[1][...] if before else None
    block = min(rows.stop - rows.start, 256)
    for start in range(rows.start, rows.stop, block):
        send = send_ref[start : start + block].reshape(1, -1)
        recv = recv_ref[start : start + block].reshape(1, -1)
        edges = edges_ref[start : start + block, :]
        senders = mm(match_rows(as_column(send), node_count), nodes).astype(BF)
        receivers = mm(match_rows(as_column(recv), node_count), nodes).astype(BF)
        stacked = jnp.concatenate([edges, senders, receivers], axis=1)
        normed = edge_tail(
            mm(stacked, win_ref[...]), wout_ref[...], *[v[layer : layer + 1, :] for v in vec_refs]
        )
        new_ref[start : start + block, :] = (edges.astype(F32) + normed).astype(BF)
        part = mm(match_columns(recv, node_count), normed.astype(BF))
        total = part if total is None else total + part
    sum_ref[...] = total


def far_first_kernel(lines, slot, *refs):
    slots, tables, win_ref = refs[0:PLANE], refs[PLANE : PLANE + 2], refs[PLANE + 2]
    out_ref, late_ref, *scatter_refs = refs[PLANE + 3 :]
    span = lines * COARSE
    for pair in range(0, PLANE, 2):
        columns_s, columns_r, rows_r = [], [], []
        for ref in slots[pair : pair + 2]:
            meta = ref[slot : slot + 16, :].astype(F32)[0:8, 0 : -(-slot // 128) * 128]
            tall = jnp.transpose(meta)[0:slot, :]
            columns_s.append((tall[:, 0:1] * COARSE + tall[:, 1:2]).astype(I32))
            columns_r.append((tall[:, 2:3] * COARSE + tall[:, 3:4]).astype(I32) - COARSE)
            rows_r.append((meta[2:3, 0:slot] * COARSE + meta[3:4, 0:slot]).astype(I32) - COARSE)
        column_s, column_r = jnp.concatenate(columns_s, axis=0), jnp.concatenate(columns_r, axis=0)
        senders = None
        for q, table in enumerate(tables):
            piece = mm(match_rows(column_s, table.shape[0], q * span), table[...])
            senders = piece if senders is None else senders + piece
        receivers = mm(match_rows(column_r, span), tables[0][...])
        edges = jnp.concatenate([ref[0:slot, :] for ref in slots[pair : pair + 2]], axis=0)
        stacked = jnp.concatenate([edges, senders.astype(BF), receivers.astype(BF)], axis=1)
        rows = slice(pair * slot, (pair + 2) * slot)
        out_ref[rows, :] = mm(stacked, win_ref[...])
        late_ref[rows, :] = match_rows(column_s, 2 * span, 2 * span)
        scatter_refs[pair // 2][...] = match_columns(jnp.concatenate(rows_r, axis=1), span)


def far_second_kernel(layer, lines, slot, keep, *refs):
    slots, refs = refs[0:PLANE], refs[PLANE:]
    straight_ref, across_ref, pre_ref, late_ref, *scatter_refs = refs[0:6]
    sum_ref, win_ref, wout_ref = refs[6:9]
    vecs, refs = [v[layer : layer + 1, :] for v in refs[9:12]], refs[12:]
    count = PLANE if keep else 3
    new_refs, own_ref, part_refs = refs[0:count], refs[count], refs[count + 1 :]
    width = pre_ref.shape[1]
    table = jnp.concatenate([straight_ref[...], across_ref[...]], axis=0)
    total = None
    for pair in range(0, PLANE, 2):
        rows = slice(pair * slot, (pair + 2) * slot)
        senders = mm(late_ref[rows, :], table).astype(BF)
        pre_act = pre_ref[rows, :] + mm(senders, win_ref[width : 2 * width, :])
        normed = edge_tail(pre_act, wout_ref[...], *vecs)
        edges = jnp.concatenate([ref[0:slot, :] for ref in slots[pair : pair + 2]], axis=0)
        new = (edges.astype(F32) + normed).astype(BF)
        for j in range(2):
            piece = new[j * slot : (j + 1) * slot, :]
            if keep:
                new_refs[pair + j][0:slot, :] = piece
                new_refs[pair + j][slot:, :] = slots[pair + j][slot:, :]
            elif j == 0:
                new_refs[pair][...] = piece
            else:
                new_refs[1][pair // 2 * slot : (pair // 2 + 1) * slot, :] = piece
        part = mm(scatter_refs[pair // 2][...], normed.astype(BF))
        total = part if total is None else total + part
    own_ref[...] = total[0:COARSE, :] + sum_ref[0:COARSE, :]
    for i, ref in enumerate(part_refs):
        ref[...] = total[(i + 1) * COARSE : (i + 2) * COARSE, :].astype(BF)


def node_update(layer, nodes, sums, win_ref, wout_ref, vec_refs):
    stacked = jnp.concatenate([nodes, sums.astype(BF)], axis=1)
    bias, gain, shift = [v[layer : layer + 1, :] for v in vec_refs]
    normed = edge_tail(mm(stacked, win_ref[layer]), wout_ref[layer], bias, gain, shift)
    return (nodes.astype(F32) + normed).astype(BF)


def rest_kernel(layer, nodes_ref, sum_ref, win_ref, wout_ref, *refs):
    sums = sum_ref[COARSE:, :]
    refs[-1][...] = node_update(layer, nodes_ref[...], sums, win_ref, wout_ref, refs[0:3])


def coarse_kernel(layer, nodes_ref, rest_ref, own_ref, *refs):
    part_refs, (win_ref, wout_ref), vec_refs, out_ref = refs[:-6], refs[-6:-4], refs[-4:-1], refs[-1]
    sums = own_ref[...]
    for ref in part_refs:
        sums = sums + ref[...].astype(F32)
    out_ref[0:COARSE, :] = node_update(layer, nodes_ref[...], sums, win_ref, wout_ref, vec_refs)
    if out_ref.shape[0] > COARSE:
        out_ref[COARSE:, :] = rest_ref[...]


def restore_kernel(slot, pos_ref, *refs):
    slots, out_ref = refs[:-1], refs[-1]
    column = as_column(pos_ref[...])
    total = None
    pieces = [slots[0][...], slots[1][0:slot, :], slots[2][0:slot, :], slots[2][slot:, :]]
    for m, rows in enumerate(pieces):
        piece = mm(match_rows(column - m * slot, slot), rows)
        total = piece if total is None else total + piece
    out_ref[...] = total.astype(BF)


def call(kernel, outs, args, flops, limit, first=None, scratch=()):
    bytes_accessed = sum(a.size * a.dtype.itemsize for a in args)
    bytes_accessed += sum(o.size * o.dtype.itemsize for o in outs)
    whole = pl.BlockSpec(memory_space=pltpu.VMEM)
    specs = [whole] * len(args)
    if first is not None:
        specs = [pl.BlockSpec(memory_space=pltpu.SMEM)] * first
        specs += [pl.BlockSpec(memory_space=pltpu.HBM)] * (len(args) - first)
        args = list(args[:first]) + [
            pltpu.with_memory_space_constraint(a, pltpu.HBM) for a in args[first:]
        ]
    return pl.pallas_call(
        kernel,
        out_shape=outs,
        in_specs=specs,
        out_specs=[whole] * len(outs),
        scratch_shapes=scratch,
        compiler_params=pltpu.CompilerParams(vmem_limit_bytes=limit),
        cost_estimate=pl.CostEstimate(flops=flops, bytes_accessed=bytes_accessed, transcendentals=0),
    )(*args)


def body(
    node_feat,
    local_edges,
    far_edges,
    local_send,
    local_recv,
    far_send,
    far_recv,
    edge_in,
    edge_out,
    node_in,
    node_out,
    edge_bias,
    edge_gain,
    edge_shift,
    node_bias,
    node_gain,
    node_shift,
):
    devices = lax.axis_size("patch")
    lines = devices // PLANE
    node_count, width = node_feat.shape
    far_count, local_count = far_edges.shape[0], local_edges.shape[0]
    slot = lines * (5 * far_count // (2 * devices))
    padded = -(-(slot + 4) // 16) * 16
    layers = edge_in.shape[0]
    limit = (24 if lines <= 4 else 56) * 2**20
    shape = jax.ShapeDtypeStruct
    place = [0] * lines
    for z in range(lines):
        place[z ^ (z >> 1)] = z

    def swap(values, distance):
        return lax.ppermute(values, "patch", [(i, i ^ distance) for i in range(devices)])

    own = lax.axis_index("patch").reshape(1).astype(I32)
    fs, fr = far_send.reshape(1, -1), far_recv.reshape(1, -1)
    tied = lax.optimization_barrier
    prepared = call(
        functools.partial(prep_kernel, node_count, lines, slot),
        [shape((1, far_count), I32), shape((COARSE, width), BF)]
        + [shape((node_count - COARSE, width), BF)]
        + [shape((padded, width), BF)] * PLANE,
        [own, fs, fr, far_edges, node_feat],
        2 * PLANE * slot * far_count * width,
        limit,
        first=1,
        scratch=[
            pltpu.VMEM((1, far_count), I32),
            pltpu.VMEM((1, far_count), I32),
            pltpu.VMEM((far_count, width), BF),
            pltpu.SemaphoreType.DMA((5,)),
        ],
    )
    pos, coarse, rest, slots = *prepared[0:3], prepared[3:]
    slots = [slots[0]] + [swap(slots[m], m) for m in range(1, PLANE)]
    def fetch(sources, picks):
        pieces = [sources[i] if layer is None else sources[i][0] for i, layer in picks]
        return call(
            functools.partial(load_kernel, picks),
            [shape(v.shape, v.dtype) for v in pieces],
            sources,
            0,
            limit,
            first=0,
            scratch=[pltpu.SemaphoreType.DMA((len(picks),))],
        )

    first = [local_edges, local_send, local_recv, edge_bias, edge_gain, edge_shift]
    picks = [(i, None) for i in range(len(first))] + [(len(first), 0), (len(first) + 1, 0)]
    first = fetch([*first, edge_in, edge_out], picks)
    far_rows, span = PLANE * slot, lines * COARSE
    cut = local_count // 3 * 2 // 256 * 256
    pieces = [slice(0, cut), slice(cut, local_count)] if cut else [slice(0, local_count)]
    hop = None
    if lines == 4:
        hop = [swap(coarse, 12), swap(coarse, 4)]
        hop, first, slots = tied((hop, first, slots))
    local, local_send, local_recv = first[0:3]
    edge_vecs, weights = first[3:6], [first[6:8]]
    for l in range(layers):
        last = l == layers - 1

        def local_part(rows, before=()):
            return call(
                functools.partial(local_kernel, l, rows),
                [shape((rows.stop, width), BF), shape((node_count, width), F32)],
                [coarse, rest, local, local_send, local_recv, *weights[l], *edge_vecs, *before],
                2 * (rows.stop - rows.start) * width * (3 * node_count + 4 * width),
                limit,
            )

        done = local_part(pieces[0])
        if lines == 4:
            z3, z1 = hop if l == 0 else (swap(coarse, 12), swap(coarse, 4))
            if l:
                z3, z1, done = tied((z3, z1, done))
            near = jnp.concatenate([coarse, z1, z3], axis=0)
            z2 = swap(z3, 4)
            across = swap(near, 2)
        else:
            near = [coarse if z == 0 else swap(coarse, PLANE * z) for z in place]
            near, z2 = jnp.concatenate(near[:-1], axis=0), near[-1]
            across = swap(near, 2)
        if l == 0:
            z2, done = tied((z2, done))
        for rows in pieces[1:]:
            done = local_part(rows, done)
        if l:
            z2, done = tied((z2, done))
        late = swap(z2, 2)
        table = jnp.concatenate([near, z2], axis=0)
        tables = [table, swap(table, 1)]
        found = call(
            functools.partial(far_first_kernel, lines, slot),
            [shape((far_rows, width), F32), shape((far_rows, 2 * span), BF)]
            + [shape((span, 2 * slot), BF)] * 2,
            [*slots, *tables, weights[l][0]],
            2 * far_rows * width * (3 * span + 3 * width),
            limit,
        )
        late, found, done = tied((late, found, done))
        local, sums = done
        late = jnp.concatenate([across, late], axis=0)
        late = [late, swap(late, 1)]
        moved = [shape((padded, width), BF)] * PLANE
        if last:
            moved = [shape((rows * slot, width), BF) for rows in (1, 2, 1)]
        far = call(
            functools.partial(far_second_kernel, l, lines, slot, not last),
            moved
            + [shape((COARSE, width), F32)]
            + [shape((COARSE, width), BF)] * (lines - 1),
            [*slots, *late, *found, sums, *weights[l], *edge_vecs],
            2 * far_rows * width * (3 * span + 2 * width),
            limit,
        )
        slots, parts = [*far[: len(moved)]], far[len(moved) :]
        if last:
            kept, paired, crossing = slots
            paired = swap(paired, 1)
            crossing = jnp.concatenate([crossing, paired[slot:]], axis=0)
            slots = [kept, paired, swap(crossing, 2)]
        far_parts = [swap(parts[i], PLANE * place[i]) for i in range(lines - 1, 0, -1)]
        parts = [parts[0], *far_parts]
        if l == 0:
            sources = [node_in, node_out, node_bias, node_gain, node_shift]
            picks = [(i, None) for i in range(len(sources))]
            for i in range(1, layers):
                picks += [(len(sources), i), (len(sources) + 1, i)]
            sources, sums = tied(([*sources, edge_in, edge_out], sums))
            second = fetch(sources, picks)
            node_in, node_out, node_vecs = *second[0:2], second[2:5]
            weights += [second[5 + 2 * i : 7 + 2 * i] for i in range(layers - 1)]
        ends = [node_in, node_out, *node_vecs]
        rest = call(
            functools.partial(rest_kernel, l),
            [shape((node_count - COARSE, width), BF)],
            [rest, sums, *ends],
            6 * (node_count - COARSE) * width * width,
            limit,
        )[0]
        coarse = call(
            functools.partial(coarse_kernel, l),
            [shape((node_count if last else COARSE, width), BF)],
            [coarse, rest, *parts, *ends],
            6 * COARSE * width * width,
            limit,
        )[0]
    far_out = call(
        functools.partial(restore_kernel, slot),
        [shape((far_count, width), BF)],
        [pos, *slots],
        2 * PLANE * slot * far_count * width,
        limit,
    )[0]
    return (coarse, local, far_out)


def solution(mesh):
    split = P(("groups", "patch"), None)
    line = P(("groups", "patch"))
    return jax.shard_map(
        body,
        mesh=mesh,
        in_specs=(split,) * 3 + (line,) * 4 + (P(),) * 10,
        out_specs=(split,) * 3,
        check_vma=False,
    )
```

```python
import functools

import jax
import jax.numpy as jnp
from jax import lax
from jax.experimental import pallas as pl
from jax.experimental.pallas import tpu as pltpu
from jax.sharding import PartitionSpec as P

COARSE = 64
PLANE = 4
BF = jnp.bfloat16
F32 = jnp.float32
I32 = jnp.int32


def mm(left, right):
    return jnp.dot(left, right, preferred_element_type=F32)


def silu(values):
    half = 0.5 * values
    return half * jnp.tanh(half) + half


def layer_norm(values, gain, shift):
    mean_value = jnp.mean(values, axis=-1, keepdims=True)
    centred = values - mean_value
    variance = jnp.mean(centred * centred, axis=-1, keepdims=True)
    return centred * lax.rsqrt(variance + 1e-05) * gain + shift


def match_rows(column, count, offset=0):
    where = lax.broadcasted_iota(I32, (column.shape[0], count), 1) + offset
    return jnp.where(where == column, 1.0, 0.0).astype(BF)


def match_columns(row, count, offset=0):
    where = lax.broadcasted_iota(I32, (count, row.shape[1]), 0) + offset
    return jnp.where(where == row, 1.0, 0.0).astype(BF)


def as_column(row):
    tall = jnp.broadcast_to(row.astype(F32), (8, row.shape[1]))
    return jnp.transpose(tall)[:, :1].astype(I32)


def bits(count):
    assert count & (count - 1) == 0
    return count.bit_length() - 1


def prep_kernel(node_count, lines, slot, own_ref, fs_hbm, fr_hbm, fe_hbm, nodes_hbm, *refs):
    pos_ref, coarse_ref, rest_ref, slot_refs = *refs[0:3], refs[3 : 3 + PLANE]
    fs_ref, fr_ref, fe_ref, sems = refs[3 + PLANE :]
    moves = [
        (fs_hbm, fs_ref),
        (fr_hbm, fr_ref),
        (fe_hbm, fe_ref),
        (nodes_hbm.at[0:COARSE, :], coarse_ref),
        (nodes_hbm.at[COARSE:, :], rest_ref),
    ]
    copies = [pltpu.make_async_copy(a, b, sems.at[i]) for i, (a, b) in enumerate(moves)]
    for copy in copies:
        copy.start()
    for copy in copies[0:3]:
        copy.wait()
    own = own_ref[0]
    own_q, own_z = own & (PLANE - 1), lax.shift_right_logical(own, bits(PLANE))
    fs, fr = fs_ref[...], fr_ref[...]
    count = fs.shape[1]
    shift = bits(node_count)
    s_patch, s_within = lax.shift_right_logical(fs, shift), fs & (node_count - 1)
    r_patch, r_within = lax.shift_right_logical(fr, shift), fr & (node_count - 1)
    r_q = r_patch & (PLANE - 1)
    member = r_q ^ own_q
    s_rel = s_patch ^ (own_z * PLANE + r_q)
    s_z = lax.shift_right_logical(s_rel, bits(PLANE))
    s_block = (s_rel & (PLANE - 1)) * lines + (s_z ^ lax.shift_right_logical(s_z, 1))
    r_z = lax.shift_right_logical(r_patch, bits(PLANE)) ^ own_z
    r_block = (r_z ^ lax.shift_right_logical(r_z, 1)) + 1
    flags = jnp.where(lax.broadcasted_iota(I32, (8, count), 0) == member, 1.0, 0.0)
    before = jnp.where(
        lax.broadcasted_iota(I32, (count, count), 0) < lax.broadcasted_iota(I32, (count, count), 1),
        1.0,
        0.0,
    ).astype(BF)
    rank = jnp.sum(flags * mm(flags.astype(BF), before), axis=0, keepdims=True)
    pos = member * slot + rank.astype(I32)
    pos_ref[...] = pos
    row_at = lax.broadcasted_iota(I32, (8, count), 0)
    meta = jnp.where(row_at == 0, s_block, 0)
    meta = jnp.where(row_at == 1, s_within, meta)
    meta = jnp.where(row_at == 2, r_block, meta)
    meta = jnp.where(row_at == 3, r_within, meta).astype(F32).astype(BF)
    for m, ref in enumerate(slot_refs):
        moved = match_columns(pos - m * slot, slot)
        ref[0:slot, :] = mm(moved, fe_ref[...]).astype(BF)
        tail = lax.dot_general(meta, moved, (((1,), (1,)), ((), ())), preferred_element_type=F32)
        ref[slot:, :] = jnp.zeros((ref.shape[0] - slot, ref.shape[1]), BF)
        ref[slot : slot + 16, 0:slot] = jnp.concatenate(
            [tail, jnp.zeros((8, slot), F32)], axis=0
        ).astype(BF)
    for copy in copies[3:]:
        copy.wait()


def load_kernel(picks, *refs):
    sources, held, sems = refs[: -len(picks) - 1], refs[-len(picks) - 1 : -1], refs[-1]
    copies = []
    for i, (which, layer) in enumerate(picks):
        source = sources[which] if layer is None else sources[which].at[layer]
        copies.append(pltpu.make_async_copy(source, held[i], sems.at[i]))
        copies[i].start()
    for copy in copies:
        copy.wait()


def edge_tail(pre_act, w_out, bias, gain, shift):
    hidden = silu(pre_act + bias).astype(BF)
    return layer_norm(mm(hidden, w_out), gain, shift)


def local_kernel(layer, rows, *refs):
    coarse_ref, rest_ref, edges_ref, send_ref, recv_ref, win_ref, wout_ref = refs[0:7]
    vec_refs, before, (new_ref, sum_ref) = refs[7:10], refs[10:-2], refs[-2:]
    nodes = jnp.concatenate([coarse_ref[...], rest_ref[...]], axis=0)
    node_count = nodes.shape[0]
    if before:
        new_ref[0 : rows.start, :] = before[0][0 : rows.start, :]
    total = before[1][...] if before else None
    block = min(rows.stop - rows.start, 256)
    for start in range(rows.start, rows.stop, block):
        send = send_ref[start : start + block].reshape(1, -1)
        recv = recv_ref[start : start + block].reshape(1, -1)
        edges = edges_ref[start : start + block, :]
        senders = mm(match_rows(as_column(send), node_count), nodes).astype(BF)
        receivers = mm(match_rows(as_column(recv), node_count), nodes).astype(BF)
        stacked = jnp.concatenate([edges, senders, receivers], axis=1)
        normed = edge_tail(
            mm(stacked, win_ref[...]), wout_ref[...], *[v[layer : layer + 1, :] for v in vec_refs]
        )
        new_ref[start : start + block, :] = (edges.astype(F32) + normed).astype(BF)
        part = mm(match_columns(recv, node_count), normed.astype(BF))
        total = part if total is None else total + part
    sum_ref[...] = total


def far_first_kernel(lines, slot, *refs):
    slots, tables, win_ref = refs[0:PLANE], refs[PLANE : PLANE + 2], refs[PLANE + 2]
    out_ref, late_ref, *scatter_refs = refs[PLANE + 3 :]
    span = lines * COARSE
    for pair in range(0, PLANE, 2):
        columns_s, columns_r, rows_r = [], [], []
        for ref in slots[pair : pair + 2]:
            meta = ref[slot : slot + 16, :].astype(F32)[0:8, 0 : -(-slot // 128) * 128]
            tall = jnp.transpose(meta)[0:slot, :]
            columns_s.append((tall[:, 0:1] * COARSE + tall[:, 1:2]).astype(I32))
            columns_r.append((tall[:, 2:3] * COARSE + tall[:, 3:4]).astype(I32) - COARSE)
            rows_r.append((meta[2:3, 0:slot] * COARSE + meta[3:4, 0:slot]).astype(I32) - COARSE)
        column_s, column_r = jnp.concatenate(columns_s, axis=0), jnp.concatenate(columns_r, axis=0)
        senders = None
        for q, table in enumerate(tables):
            piece = mm(match_rows(column_s, table.shape[0], q * span), table[...])
            senders = piece if senders is None else senders + piece
        receivers = mm(match_rows(column_r, span), tables[0][...])
        edges = jnp.concatenate([ref[0:slot, :] for ref in slots[pair : pair + 2]], axis=0)
        stacked = jnp.concatenate([edges, senders.astype(BF), receivers.astype(BF)], axis=1)
        rows = slice(pair * slot, (pair + 2) * slot)
        out_ref[rows, :] = mm(stacked, win_ref[...])
        late_ref[rows, :] = match_rows(column_s, 2 * span, 2 * span)
        scatter_refs[pair // 2][...] = match_columns(jnp.concatenate(rows_r, axis=1), span)


def far_second_kernel(layer, lines, slot, pairs, chained, keep, *refs):
    count = 2 * len(pairs)
    slots, refs = refs[0:count], refs[count:]
    straight_ref, across_ref, pre_ref, late_ref, *scatter_refs = refs[0:6]
    total, refs = (refs[6][...], refs[7:]) if chained else (None, refs[6:])
    win_ref, wout_ref = refs[0:2]
    vecs, refs = [v[layer : layer + 1, :] for v in refs[2:5]], refs[5:]
    new_refs, sum_refs = refs[0:count], refs[count:]
    width = pre_ref.shape[1]
    table = jnp.concatenate([straight_ref[...], across_ref[...]], axis=0)
    for i, pair in enumerate(pairs):
        rows, own = slice(pair * slot, (pair + 2) * slot), slots[2 * i : 2 * i + 2]
        senders = mm(late_ref[rows, :], table).astype(BF)
        pre_act = pre_ref[rows, :] + mm(senders, win_ref[width : 2 * width, :])
        normed = edge_tail(pre_act, wout_ref[...], *vecs)
        edges = jnp.concatenate([ref[0:slot, :] for ref in own], axis=0)
        new = (edges.astype(F32) + normed).astype(BF)
        for j in range(2):
            new_refs[2 * i + j][0:slot, :] = new[j * slot : (j + 1) * slot, :]
            if keep:
                new_refs[2 * i + j][slot:, :] = own[j][slot:, :]
        part = mm(scatter_refs[pair // 2][...], normed.astype(BF))
        total = part if total is None else total + part
    if len(sum_refs) == 1:
        sum_refs[0][...] = total
        return
    sum_refs[0][...] = total[0:COARSE, :]
    for i, ref in enumerate(sum_refs[1:]):
        ref[...] = total[(i + 1) * COARSE : (i + 2) * COARSE, :].astype(BF)


def node_update(layer, nodes, sums, win_ref, wout_ref, vec_refs):
    stacked = jnp.concatenate([nodes, sums.astype(BF)], axis=1)
    bias, gain, shift = [v[layer : layer + 1, :] for v in vec_refs]
    normed = edge_tail(mm(stacked, win_ref[layer]), wout_ref[layer], bias, gain, shift)
    return (nodes.astype(F32) + normed).astype(BF)


def rest_kernel(layer, nodes_ref, sum_ref, win_ref, wout_ref, *refs):
    sums = sum_ref[COARSE:, :]
    new = node_update(layer, nodes_ref[...], sums, win_ref, wout_ref, refs[0:3])
    if len(refs) == 4:
        refs[3][...] = new
        return
    pos_ref, out_ref, back_ref = refs[3:]
    out_ref[...] = new
    back_ref[...] = match_rows(as_column(pos_ref[...]), back_ref.shape[1])


def coarse_kernel(layer, lines, nodes_ref, sum_ref, *refs):
    part_refs, refs = refs[0:lines], refs[lines:]
    (win_ref, wout_ref), vec_refs, refs = refs[0:2], refs[2:5], refs[5:]
    if len(refs) > 1:
        rest_ref, back_ref, *slot_refs, out_ref, far_ref = refs
        slots = jnp.concatenate([ref[...] for ref in slot_refs], axis=0)
        far_ref[...] = mm(back_ref[...], slots).astype(BF)
        out_ref[COARSE:, :] = rest_ref[...]
    else:
        out_ref = refs[0]
    sums = sum_ref[0:COARSE, :] + part_refs[0][...]
    for ref in part_refs[1:]:
        sums = sums + ref[...].astype(F32)
    out_ref[0:COARSE, :] = node_update(layer, nodes_ref[...], sums, win_ref, wout_ref, vec_refs)


def call(kernel, outs, args, flops, limit, first=None, scratch=()):
    bytes_accessed = sum(a.size * a.dtype.itemsize for a in [*args, *outs]) if flops or first == 0 else 0
    whole = pl.BlockSpec(memory_space=pltpu.VMEM)
    specs = [whole] * len(args)
    if first is not None:
        specs = [pl.BlockSpec(memory_space=pltpu.SMEM)] * first
        specs += [pl.BlockSpec(memory_space=pltpu.HBM)] * (len(args) - first)
        args = list(args[:first]) + [
            pltpu.with_memory_space_constraint(a, pltpu.HBM) for a in args[first:]
        ]
    return pl.pallas_call(
        kernel,
        out_shape=outs,
        in_specs=specs,
        out_specs=[whole] * len(outs),
        scratch_shapes=scratch,
        compiler_params=pltpu.CompilerParams(vmem_limit_bytes=limit),
        cost_estimate=pl.CostEstimate(flops=flops, bytes_accessed=bytes_accessed, transcendentals=0),
    )(*args)


def body(
    node_feat,
    local_edges,
    far_edges,
    local_send,
    local_recv,
    far_send,
    far_recv,
    edge_in,
    edge_out,
    node_in,
    node_out,
    edge_bias,
    edge_gain,
    edge_shift,
    node_bias,
    node_gain,
    node_shift,
):
    devices = lax.axis_size("patch")
    lines = devices // PLANE
    node_count, width = node_feat.shape
    far_count, local_count = far_edges.shape[0], local_edges.shape[0]
    slot = lines * (5 * far_count // (2 * devices))
    padded = -(-(slot + 4) // 16) * 16
    layers = edge_in.shape[0]
    limit = (24 if lines <= 4 else 56) * 2**20
    shape = jax.ShapeDtypeStruct
    place = [0] * lines
    for z in range(lines):
        place[z ^ (z >> 1)] = z

    def swap(values, distance):
        return lax.ppermute(values, "patch", [(i, i ^ distance) for i in range(devices)])

    own = lax.axis_index("patch").reshape(1).astype(I32)
    fs, fr = far_send.reshape(1, -1), far_recv.reshape(1, -1)
    tied = lax.optimization_barrier
    prepared = call(
        functools.partial(prep_kernel, node_count, lines, slot),
        [shape((1, far_count), I32), shape((COARSE, width), BF)]
        + [shape((node_count - COARSE, width), BF)]
        + [shape((padded, width), BF)] * PLANE,
        [own, fs, fr, far_edges, node_feat],
        2 * PLANE * slot * far_count * width,
        limit,
        first=1,
        scratch=[
            pltpu.VMEM((1, far_count), I32),
            pltpu.VMEM((1, far_count), I32),
            pltpu.VMEM((far_count, width), BF),
            pltpu.SemaphoreType.DMA((5,)),
        ],
    )
    pos, coarse, rest, slots = *prepared[0:3], prepared[3:]
    slots = [slots[0]] + [swap(slots[m], m) for m in range(1, PLANE)]
    def fetch(sources, picks):
        pieces = [sources[i] if layer is None else sources[i][0] for i, layer in picks]
        return call(
            functools.partial(load_kernel, picks),
            [shape(v.shape, v.dtype) for v in pieces],
            sources,
            0,
            limit,
            first=0,
            scratch=[pltpu.SemaphoreType.DMA((len(picks),))],
        )

    first = [local_edges, local_send, local_recv, edge_bias, edge_gain, edge_shift]
    picks = [(i, None) for i in range(len(first))] + [(len(first), 0), (len(first) + 1, 0)]
    first = fetch([*first, edge_in, edge_out], picks)
    far_rows, span = PLANE * slot, lines * COARSE
    cut = local_count // 3 * 2 // 256 * 256
    pieces = [slice(0, cut), slice(cut, local_count)] if cut else [slice(0, local_count)]
    local, local_send, local_recv = first[0:3]
    edge_vecs, weights = first[3:6], [first[6:8]]
    for l in range(layers):
        last = l == layers - 1

        def local_part(rows, before=(), share=1):
            return call(
                functools.partial(local_kernel, l, rows),
                [shape((rows.stop, width), BF), shape((node_count, width), F32)],
                [coarse, rest, local, local_send, local_recv, *weights[l], *edge_vecs, *before],
                2 * (rows.stop - rows.start) * width * (3 * node_count + 4 * width) * share,
                limit,
            )

        done = local_part(pieces[0], share=min(l, 1))
        if lines == 4:
            z3, z1 = swap(coarse, 12), swap(coarse, 4)
            if l:
                z3, z1, done = tied((z3, z1, done))
            else:
                z3, z1, done, slots = tied((z3, z1, done, slots))
            near = jnp.concatenate([coarse, z1, z3], axis=0)
            z2 = swap(z3, 4)
            across = swap(near, 2)
        else:
            near = [coarse if z == 0 else swap(coarse, PLANE * z) for z in place]
            near, z2 = jnp.concatenate(near[:-1], axis=0), near[-1]
            across = swap(near, 2)
        if not last:
            z2, done = tied((z2, done))
            for rows in pieces[1:]:
                done = local_part(rows, done)
        late = swap(z2, 2)
        table = jnp.concatenate([near, z2], axis=0)
        tables = [table, swap(table, 1)]
        found = call(
            functools.partial(far_first_kernel, lines, slot),
            [shape((far_rows, width), F32), shape((far_rows, 2 * span), BF)]
            + [shape((span, 2 * slot), BF)] * 2,
            [*slots, *tables, weights[l][0]],
            2 * far_rows * width * (3 * span + 3 * width),
            limit,
        )
        late, found, done = tied((late, found, done))
        late = jnp.concatenate([across, late], axis=0)
        late = [late, swap(late, 1)]
        moved = shape((slot if last else padded, width), BF)
        parts_shape = [shape((COARSE, width), F32)] + [shape((COARSE, width), BF)] * (lines - 1)

        def far_part(pairs, before, outs):
            return call(
                functools.partial(far_second_kernel, l, lines, slot, pairs, len(before) > 0, not last),
                [moved] * (2 * len(pairs)) + outs,
                [*[v for i in pairs for v in slots[i : i + 2]], *late, *found, *before]
                + [*weights[l], *edge_vecs],
                4 * len(pairs) * slot * width * (3 * span + 2 * width),
                limit,
            )

        if last:
            ahead = far_part((2,), [], [shape((span, width), F32)])
            passed = swap(ahead[1], 1)
            passed, far = tied((passed, far_part((0,), [ahead[2]], parts_shape)))
            crossing = jnp.concatenate([ahead[0], passed], axis=0)
            slots, parts = [far[0], swap(far[1], 1), swap(crossing, 2)], far[2:]
            parts, done = tied((parts, done))
            for rows in pieces[1:]:
                done = local_part(rows, done)
        else:
            far = far_part((0, 2), [], parts_shape)
            slots, parts = [*far[:PLANE]], far[PLANE:]
        local, sums = done
        far_parts = [swap(parts[i], PLANE * place[i]) for i in range(lines - 1, 0, -1)]
        parts = [parts[0], *far_parts]
        if l == 0:
            sources = [node_in, node_out, node_bias, node_gain, node_shift]
            picks = [(i, None) for i in range(len(sources))]
            for i in range(1, layers):
                picks += [(len(sources), i), (len(sources) + 1, i)]
            sources, sums = tied(([*sources, edge_in, edge_out], sums))
            second = fetch(sources, picks)
            node_in, node_out, node_vecs = *second[0:2], second[2:5]
            weights += [second[5 + 2 * i : 7 + 2 * i] for i in range(layers - 1)]
        ends = [node_in, node_out, *node_vecs]
        rest = call(
            functools.partial(rest_kernel, l),
            [shape((node_count - COARSE, width), BF)]
            + [shape((far_count, far_rows), BF)] * last,
            [rest, sums, *ends] + [pos] * last,
            6 * (node_count - COARSE) * width * width,
            limit,
        )
        if last:
            return_shapes = [shape((node_count, width), BF), shape((far_count, width), BF)]
            extra = [*rest, *slots]
        else:
            return_shapes, extra, rest = [shape((COARSE, width), BF)], [], rest[0]
        coarse, *far_out = call(
            functools.partial(coarse_kernel, l, lines),
            return_shapes,
            [coarse, sums, *parts, *ends, *extra],
            6 * COARSE * width * width,
            limit,
        )
    return (coarse, local, far_out[0])


def solution(mesh):
    split = P(("groups", "patch"), None)
    line = P(("groups", "patch"))
    return jax.shard_map(
        body,
        mesh=mesh,
        in_specs=(split,) * 3 + (line,) * 4 + (P(),) * 10,
        out_specs=(split,) * 3,
        check_vma=False,
    )
```

```python
import functools

import jax
import jax.numpy as jnp
from jax import lax
from jax.experimental import pallas as pl
from jax.experimental.pallas import tpu as pltpu
from jax.sharding import PartitionSpec as P

COARSE = 64
PLANE = 4
BF = jnp.bfloat16
F32 = jnp.float32
I32 = jnp.int32


def mm(left, right):
    return jnp.dot(left, right, preferred_element_type=F32)


def silu(values):
    half = 0.5 * values
    return half * jnp.tanh(half) + half


def layer_norm(values, gain, shift):
    mean_value = jnp.mean(values, axis=-1, keepdims=True)
    centred = values - mean_value
    variance = jnp.mean(centred * centred, axis=-1, keepdims=True)
    return centred * lax.rsqrt(variance + 1e-05) * gain + shift


def match_rows(column, count, offset=0):
    where = lax.broadcasted_iota(I32, (column.shape[0], count), 1) + offset
    return jnp.where(where == column, 1.0, 0.0).astype(BF)


def match_columns(row, count, offset=0):
    where = lax.broadcasted_iota(I32, (count, row.shape[1]), 0) + offset
    return jnp.where(where == row, 1.0, 0.0).astype(BF)


def as_column(row):
    tall = jnp.broadcast_to(row.astype(F32), (8, row.shape[1]))
    return jnp.transpose(tall)[:, :1].astype(I32)


def bits(count):
    assert count & (count - 1) == 0
    return count.bit_length() - 1


def prep_kernel(node_count, lines, slot, own_ref, fs_hbm, fr_hbm, fe_hbm, nodes_hbm, *refs):
    pos_ref, coarse_ref, rest_ref, slot_refs = *refs[0:3], refs[3 : 3 + PLANE]
    fs_ref, fr_ref, fe_ref, sems = refs[3 + PLANE :]
    moves = [
        (fs_hbm, fs_ref),
        (fr_hbm, fr_ref),
        (fe_hbm, fe_ref),
        (nodes_hbm.at[0:COARSE, :], coarse_ref),
        (nodes_hbm.at[COARSE:, :], rest_ref),
    ]
    copies = [pltpu.make_async_copy(a, b, sems.at[i]) for i, (a, b) in enumerate(moves)]
    for copy in copies:
        copy.start()
    for copy in copies[0:3]:
        copy.wait()
    own = own_ref[0]
    own_q, own_z = own & (PLANE - 1), lax.shift_right_logical(own, bits(PLANE))
    fs, fr = fs_ref[...], fr_ref[...]
    count = fs.shape[1]
    shift = bits(node_count)
    s_patch, s_within = lax.shift_right_logical(fs, shift), fs & (node_count - 1)
    r_patch, r_within = lax.shift_right_logical(fr, shift), fr & (node_count - 1)
    r_q = r_patch & (PLANE - 1)
    member = r_q ^ own_q
    s_rel = s_patch ^ (own_z * PLANE + r_q)
    s_z = lax.shift_right_logical(s_rel, bits(PLANE))
    s_block = (s_rel & (PLANE - 1)) * lines + (s_z ^ lax.shift_right_logical(s_z, 1))
    r_z = lax.shift_right_logical(r_patch, bits(PLANE)) ^ own_z
    r_block = (r_z ^ lax.shift_right_logical(r_z, 1)) + 1
    flags = jnp.where(lax.broadcasted_iota(I32, (8, count), 0) == member, 1.0, 0.0)
    before = jnp.where(
        lax.broadcasted_iota(I32, (count, count), 0) < lax.broadcasted_iota(I32, (count, count), 1),
        1.0,
        0.0,
    ).astype(BF)
    rank = jnp.sum(flags * mm(flags.astype(BF), before), axis=0, keepdims=True)
    pos = member * slot + rank.astype(I32)
    pos_ref[...] = pos
    row_at = lax.broadcasted_iota(I32, (8, count), 0)
    meta = jnp.where(row_at == 0, s_block, 0)
    meta = jnp.where(row_at == 1, s_within, meta)
    meta = jnp.where(row_at == 2, r_block, meta)
    meta = jnp.where(row_at == 3, r_within, meta).astype(F32).astype(BF)
    for m, ref in enumerate(slot_refs):
        moved = match_columns(pos - m * slot, slot)
        ref[0:slot, :] = mm(moved, fe_ref[...]).astype(BF)
        tail = lax.dot_general(meta, moved, (((1,), (1,)), ((), ())), preferred_element_type=F32)
        ref[slot:, :] = jnp.zeros((ref.shape[0] - slot, ref.shape[1]), BF)
        ref[slot : slot + 16, 0:slot] = jnp.concatenate(
            [tail, jnp.zeros((8, slot), F32)], axis=0
        ).astype(BF)
    for copy in copies[3:]:
        copy.wait()


def load_kernel(picks, *refs):
    sources, held, sems = refs[: -len(picks) - 1], refs[-len(picks) - 1 : -1], refs[-1]
    copies = []
    for i, (which, layer) in enumerate(picks):
        source = sources[which] if layer is None else sources[which].at[layer]
        copies.append(pltpu.make_async_copy(source, held[i], sems.at[i]))
        copies[i].start()
    for copy in copies:
        copy.wait()


def edge_tail(pre_act, w_out, bias, gain, shift):
    hidden = silu(pre_act + bias).astype(BF)
    return layer_norm(mm(hidden, w_out), gain, shift)


def local_kernel(layer, rows, *refs):
    coarse_ref, rest_ref, edges_ref, send_ref, recv_ref, win_ref, wout_ref = refs[0:7]
    vec_refs, before, (new_ref, sum_ref) = refs[7:10], refs[10:-2], refs[-2:]
    nodes = jnp.concatenate([coarse_ref[...], rest_ref[...]], axis=0)
    node_count = nodes.shape[0]
    if before:
        new_ref[0 : rows.start, :] = before[0][0 : rows.start, :]
    total = before[1][...] if before else None
    block = min(rows.stop - rows.start, 256)
    for start in range(rows.start, rows.stop, block):
        send = send_ref[start : start + block].reshape(1, -1)
        recv = recv_ref[start : start + block].reshape(1, -1)
        edges = edges_ref[start : start + block, :]
        senders = mm(match_rows(as_column(send), node_count), nodes).astype(BF)
        receivers = mm(match_rows(as_column(recv), node_count), nodes).astype(BF)
        stacked = jnp.concatenate([edges, senders, receivers], axis=1)
        normed = edge_tail(
            mm(stacked, win_ref[...]), wout_ref[...], *[v[layer : layer + 1, :] for v in vec_refs]
        )
        new_ref[start : start + block, :] = (edges.astype(F32) + normed).astype(BF)
        part = mm(match_columns(recv, node_count), normed.astype(BF))
        total = part if total is None else total + part
    sum_ref[...] = total


def far_first_kernel(lines, slot, *refs):
    slots, tables, win_ref = refs[0:PLANE], refs[PLANE : PLANE + 2], refs[PLANE + 2]
    out_ref, late_ref, *scatter_refs = refs[PLANE + 3 :]
    span, size = lines * COARSE, PLANE // len(scatter_refs)
    columns_s, columns_r, rows_r = [], [], []
    for ref in slots:
        meta = ref[slot : slot + 16, :].astype(F32)[0:8, 0 : -(-slot // 128) * 128]
        tall = jnp.transpose(meta)[0:slot, :]
        columns_s.append((tall[:, 0:1] * COARSE + tall[:, 1:2]).astype(I32))
        columns_r.append((tall[:, 2:3] * COARSE + tall[:, 3:4]).astype(I32) - COARSE)
        rows_r.append((meta[2:3, 0:slot] * COARSE + meta[3:4, 0:slot]).astype(I32) - COARSE)
    column_s, column_r = jnp.concatenate(columns_s, axis=0), jnp.concatenate(columns_r, axis=0)
    senders = None
    for q, table in enumerate(tables):
        piece = mm(match_rows(column_s, span, q * span), table[...])
        senders = piece if senders is None else senders + piece
    receivers = mm(match_rows(column_r, span), tables[0][...])
    edges = jnp.concatenate([ref[0:slot, :] for ref in slots], axis=0)
    stacked = jnp.concatenate([edges, senders.astype(BF), receivers.astype(BF)], axis=1)
    out_ref[...] = mm(stacked, win_ref[...])
    late_ref[...] = match_rows(column_s, 2 * span, 2 * span)
    for i, ref in enumerate(scatter_refs):
        ref[...] = match_columns(jnp.concatenate(rows_r[i * size : (i + 1) * size], axis=1), span)


def far_second_kernel(layer, lines, slot, start, chained, keep, *refs):
    straight_ref, across_ref, pre_ref, late_ref, scatter_ref, *refs = refs
    total, refs = (refs[0][...], refs[1:]) if chained else (None, refs)
    win_ref, wout_ref = refs[0:2]
    vecs, refs = [v[layer : layer + 1, :] for v in refs[2:5]], refs[5:]
    count = scatter_ref.shape[1] // slot
    slots, new_refs, sum_refs = refs[0:count], refs[count : 2 * count], refs[2 * count :]
    rows, width = slice(start * slot, (start + count) * slot), pre_ref.shape[1]
    table = jnp.concatenate([straight_ref[...], across_ref[...]], axis=0)
    senders = mm(late_ref[rows, :], table).astype(BF)
    pre_act = pre_ref[rows, :] + mm(senders, win_ref[width : 2 * width, :])
    normed = edge_tail(pre_act, wout_ref[...], *vecs)
    edges = jnp.concatenate([ref[0:slot, :] for ref in slots], axis=0)
    new = (edges.astype(F32) + normed).astype(BF)
    for j in range(count):
        new_refs[j][0:slot, :] = new[j * slot : (j + 1) * slot, :]
        if keep:
            new_refs[j][slot:, :] = slots[j][slot:, :]
    part = mm(scatter_ref[...], normed.astype(BF))
    total = part if total is None else total + part
    if len(sum_refs) == 1:
        sum_refs[0][...] = total
        return
    sum_refs[0][...] = total[0:COARSE, :]
    for i, ref in enumerate(sum_refs[1:]):
        ref[...] = total[(i + 1) * COARSE : (i + 2) * COARSE, :].astype(BF)


def node_update(layer, nodes, sums, win_ref, wout_ref, vec_refs):
    stacked = jnp.concatenate([nodes, sums.astype(BF)], axis=1)
    bias, gain, shift = [v[layer : layer + 1, :] for v in vec_refs]
    normed = edge_tail(mm(stacked, win_ref[layer]), wout_ref[layer], bias, gain, shift)
    return (nodes.astype(F32) + normed).astype(BF)


def rest_kernel(layer, nodes_ref, sum_ref, win_ref, wout_ref, *refs):
    sums = sum_ref[COARSE:, :]
    new = node_update(layer, nodes_ref[...], sums, win_ref, wout_ref, refs[0:3])
    if len(refs) == 4:
        refs[3][...] = new
        return
    pos_ref, *slot_refs, out_ref, half_ref, back_ref = refs[3:]
    out_ref[...] = new
    column, count = as_column(pos_ref[...]), back_ref.shape[1]
    slots = jnp.concatenate([ref[...] for ref in slot_refs], axis=0)
    half_ref[...] = mm(match_rows(column, count), slots).astype(BF)
    back_ref[...] = match_rows(column, count, count)


def coarse_kernel(layer, lines, nodes_ref, sum_ref, *refs):
    part_refs, refs = refs[0:lines], refs[lines:]
    (win_ref, wout_ref), vec_refs, refs = refs[0:2], refs[2:5], refs[5:]
    copies = []
    if len(refs) > 1:
        rest_ref, half_ref, back_ref, *slot_refs, out_hbm, far_hbm, out_ref, far_ref, sems = refs
        copies.append(pltpu.make_async_copy(rest_ref, out_hbm.at[COARSE:, :], sems.at[0]))
        copies[0].start()
        slots = jnp.concatenate([ref[...] for ref in slot_refs], axis=0)
        far_ref[...] = (half_ref[...].astype(F32) + mm(back_ref[...], slots)).astype(BF)
        copies.append(pltpu.make_async_copy(far_ref, far_hbm, sems.at[1]))
        copies[1].start()
    else:
        out_ref = refs[0]
    sums = sum_ref[0:COARSE, :] + part_refs[0][...]
    for ref in part_refs[1:]:
        sums = sums + ref[...].astype(F32)
    out_ref[...] = node_update(layer, nodes_ref[...], sums, win_ref, wout_ref, vec_refs)
    if copies:
        copies.append(pltpu.make_async_copy(out_ref, out_hbm.at[0:COARSE, :], sems.at[2]))
        copies[2].start()
        for copy in copies:
            copy.wait()


def call(kernel, outs, args, flops, limit, first=None, scratch=(), placed=pltpu.VMEM):
    bytes_accessed = sum(a.size * a.dtype.itemsize for a in [*args, *outs]) if flops or first == 0 else 0
    whole = pl.BlockSpec(memory_space=pltpu.VMEM)
    specs = [whole] * len(args)
    if first is not None:
        specs = [pl.BlockSpec(memory_space=pltpu.SMEM)] * first
        specs += [pl.BlockSpec(memory_space=pltpu.HBM)] * (len(args) - first)
        args = list(args[:first]) + [
            pltpu.with_memory_space_constraint(a, pltpu.HBM) for a in args[first:]
        ]
    return pl.pallas_call(
        kernel,
        out_shape=outs,
        in_specs=specs,
        out_specs=[pl.BlockSpec(memory_space=placed)] * len(outs),
        scratch_shapes=scratch,
        compiler_params=pltpu.CompilerParams(vmem_limit_bytes=limit),
        cost_estimate=pl.CostEstimate(flops=flops, bytes_accessed=bytes_accessed, transcendentals=0),
    )(*args)


def body(
    node_feat,
    local_edges,
    far_edges,
    local_send,
    local_recv,
    far_send,
    far_recv,
    edge_in,
    edge_out,
    node_in,
    node_out,
    edge_bias,
    edge_gain,
    edge_shift,
    node_bias,
    node_gain,
    node_shift,
):
    devices = lax.axis_size("patch")
    lines = devices // PLANE
    node_count, width = node_feat.shape
    far_count, local_count = far_edges.shape[0], local_edges.shape[0]
    slot = lines * (5 * far_count // (2 * devices))
    padded = -(-(slot + 4) // 16) * 16
    layers = edge_in.shape[0]
    limit = (24 if lines <= 4 else 56) * 2**20
    shape = jax.ShapeDtypeStruct
    place = [0] * lines
    for z in range(lines):
        place[z ^ (z >> 1)] = z

    def swap(values, distance):
        return lax.ppermute(values, "patch", [(i, i ^ distance) for i in range(devices)])

    own = lax.axis_index("patch").reshape(1).astype(I32)
    fs, fr = far_send.reshape(1, -1), far_recv.reshape(1, -1)
    tied = lax.optimization_barrier
    prepared = call(
        functools.partial(prep_kernel, node_count, lines, slot),
        [shape((1, far_count), I32), shape((COARSE, width), BF)]
        + [shape((node_count - COARSE, width), BF)]
        + [shape((padded, width), BF)] * PLANE,
        [own, fs, fr, far_edges, node_feat],
        2 * PLANE * slot * far_count * width,
        limit,
        first=1,
        scratch=[
            pltpu.VMEM((1, far_count), I32),
            pltpu.VMEM((1, far_count), I32),
            pltpu.VMEM((far_count, width), BF),
            pltpu.SemaphoreType.DMA((5,)),
        ],
    )
    pos, coarse, rest, slots = *prepared[0:3], prepared[3:]
    slots = [slots[0]] + [swap(slots[m], m) for m in range(1, PLANE)]
    def fetch(sources, picks):
        pieces = [sources[i] if layer is None else sources[i][0] for i, layer in picks]
        return call(
            functools.partial(load_kernel, picks),
            [shape(v.shape, v.dtype) for v in pieces],
            sources,
            0,
            limit,
            first=0,
            scratch=[pltpu.SemaphoreType.DMA((len(picks),))],
        )

    first = [local_edges, local_send, local_recv, edge_bias, edge_gain, edge_shift]
    picks = [(i, None) for i in range(len(first))] + [(len(first), 0), (len(first) + 1, 0)]
    first = fetch([*first, edge_in, edge_out], picks)
    far_rows, span = PLANE * slot, lines * COARSE
    cut = local_count // 3 * 2 // 256 * 256
    pieces = [slice(0, cut), slice(cut, local_count)] if cut else [slice(0, local_count)]
    local, local_send, local_recv = first[0:3]
    edge_vecs, weights = first[3:6], [first[6:8]]
    for l in range(layers):
        last = l == layers - 1

        def local_part(rows, before=(), share=1):
            return call(
                functools.partial(local_kernel, l, rows),
                [shape((rows.stop, width), BF), shape((node_count, width), F32)],
                [coarse, rest, local, local_send, local_recv, *weights[l], *edge_vecs, *before],
                2 * (rows.stop - rows.start) * width * (3 * node_count + 4 * width) * share,
                limit,
            )

        done = local_part(pieces[0], share=min(l, 1))
        if lines == 4:
            z3, z1 = swap(coarse, 12), swap(coarse, 4)
            if l:
                z3, z1, done = tied((z3, z1, done))
            else:
                z3, z1, done, slots = tied((z3, z1, done, slots))
            near = jnp.concatenate([coarse, z1, z3], axis=0)
            z2 = swap(z3, 4)
            across = swap(near, 2)
        else:
            near = [coarse if z == 0 else swap(coarse, PLANE * z) for z in place]
            near, z2 = jnp.concatenate(near[:-1], axis=0), near[-1]
            across = swap(near, 2)
        if not last:
            z2, done = tied((z2, done))
            for rows in pieces[1:]:
                done = local_part(rows, done)
        late = swap(z2, 2)
        table = jnp.concatenate([near, z2], axis=0)
        tables = [table, swap(table, 1)]
        found = call(
            functools.partial(far_first_kernel, lines, slot),
            [shape((far_rows, width), F32), shape((far_rows, 2 * span), BF)]
            + [shape((span, far_rows), BF)],
            [*slots, *tables, weights[l][0]],
            2 * far_rows * width * (3 * span + 3 * width),
            limit,
        )
        late, found, done = tied((late, found, done))
        late = jnp.concatenate([across, late], axis=0)
        late = [late, swap(late, 1)]
        moved = shape((slot if last else padded, width), BF)
        parts_shape = [shape((COARSE, width), F32)] + [shape((COARSE, width), BF)] * (lines - 1)

        def far_part(start, size, before, outs):
            return call(
                functools.partial(far_second_kernel, l, lines, slot, start, len(before) > 0, not last),
                [moved] * size + outs,
                [*late, *found[0:2], found[2 + start // size], *before]
                + [*weights[l], *edge_vecs, *slots[start : start + size]],
                2 * size * slot * width * (3 * span + 2 * width),
                limit,
            )

        far = far_part(0, PLANE, [], parts_shape)
        slots, parts = [*far[:PLANE]], far[PLANE:]
        if last:
            slots = [slots[0]] + [swap(slots[m], m) for m in range(1, PLANE)]
            parts, done = tied((parts, done))
            for rows in pieces[1:]:
                done = local_part(rows, done)
        local, sums = done
        far_parts = [swap(parts[i], PLANE * place[i]) for i in range(lines - 1, 0, -1)]
        parts = [parts[0], *far_parts]
        if l == 0:
            sources = [node_in, node_out, node_bias, node_gain, node_shift]
            picks = [(i, None) for i in range(len(sources))]
            for i in range(1, layers):
                picks += [(len(sources), i), (len(sources) + 1, i)]
            sources, sums = tied(([*sources, edge_in, edge_out], sums))
            second = fetch(sources, picks)
            node_in, node_out, node_vecs = *second[0:2], second[2:5]
            weights += [second[5 + 2 * i : 7 + 2 * i] for i in range(layers - 1)]
        ends = [node_in, node_out, *node_vecs]
        rest = call(
            functools.partial(rest_kernel, l),
            [shape((node_count - COARSE, width), BF)]
            + [shape((far_count, width), BF), shape((far_count, 2 * slot), BF)] * last,
            [rest, sums, *ends] + [pos, *slots[0:2]] * last,
            6 * (node_count - COARSE) * width * width,
            limit,
        )
        if last:
            return_shapes = [shape((node_count, width), BF), shape((far_count, width), BF)]
            extra = [*rest, *slots[2:]]
            scratch = [pltpu.VMEM((COARSE, width), BF), pltpu.VMEM((far_count, width), BF)]
            scratch += [pltpu.SemaphoreType.DMA((3,))]
        else:
            return_shapes, extra, rest = [shape((COARSE, width), BF)], [], rest[0]
        coarse, *far_out = call(
            functools.partial(coarse_kernel, l, lines),
            return_shapes,
            [coarse, sums, *parts, *ends, *extra],
            6 * COARSE * width * width,
            limit,
            scratch=scratch if last else (),
            placed=pltpu.HBM if last else pltpu.VMEM,
        )
    return (coarse, local, far_out[0])


def solution(mesh):
    split = P(("groups", "patch"), None)
    line = P(("groups", "patch"))
    return jax.shard_map(
        body,
        mesh=mesh,
        in_specs=(split,) * 3 + (line,) * 4 + (P(),) * 10,
        out_specs=(split,) * 3,
        check_vma=False,
    )
```

```python
import functools

import jax
import jax.numpy as jnp
from jax import lax
from jax.experimental import pallas as pl
from jax.experimental.pallas import tpu as pltpu
from jax.sharding import PartitionSpec as P

COARSE = 64
PLANE = 4
BF = jnp.bfloat16
F32 = jnp.float32
I32 = jnp.int32


def mm(left, right):
    return jnp.dot(left, right, preferred_element_type=F32)


def silu(values):
    half = 0.5 * values
    return half * jnp.tanh(half) + half


def layer_norm(values, gain, shift):
    mean_value = jnp.mean(values, axis=-1, keepdims=True)
    centred = values - mean_value
    variance = jnp.mean(centred * centred, axis=-1, keepdims=True)
    return centred * lax.rsqrt(variance + 1e-05) * gain + shift


def match_rows(column, count, offset=0):
    where = lax.broadcasted_iota(I32, (column.shape[0], count), 1) + offset
    return jnp.where(where == column, 1.0, 0.0).astype(BF)


def match_columns(row, count, offset=0):
    where = lax.broadcasted_iota(I32, (count, row.shape[1]), 0) + offset
    return jnp.where(where == row, 1.0, 0.0).astype(BF)


def as_column(row):
    tall = jnp.broadcast_to(row.astype(F32), (8, row.shape[1]))
    return jnp.transpose(tall)[:, :1].astype(I32)


def bits(count):
    assert count & (count - 1) == 0
    return count.bit_length() - 1


def prep_kernel(node_count, lines, slot, own_ref, fs_hbm, fr_hbm, fe_hbm, nodes_hbm, *refs):
    pos_ref, coarse_ref, rest_ref, slot_refs = *refs[0:3], refs[3 : 3 + PLANE]
    fs_ref, fr_ref, fe_ref, sems = refs[3 + PLANE :]
    moves = [
        (fs_hbm, fs_ref),
        (fr_hbm, fr_ref),
        (fe_hbm, fe_ref),
        (nodes_hbm.at[0:COARSE, :], coarse_ref),
        (nodes_hbm.at[COARSE:, :], rest_ref),
    ]
    copies = [pltpu.make_async_copy(a, b, sems.at[i]) for i, (a, b) in enumerate(moves)]
    for copy in copies:
        copy.start()
    for copy in copies[0:3]:
        copy.wait()
    own = own_ref[0]
    own_q, own_z = own & (PLANE - 1), lax.shift_right_logical(own, bits(PLANE))
    fs, fr = fs_ref[...], fr_ref[...]
    count = fs.shape[1]
    shift = bits(node_count)
    s_patch, s_within = lax.shift_right_logical(fs, shift), fs & (node_count - 1)
    r_patch, r_within = lax.shift_right_logical(fr, shift), fr & (node_count - 1)
    r_q = r_patch & (PLANE - 1)
    member = r_q ^ own_q
    s_rel = s_patch ^ (own_z * PLANE + r_q)
    s_z = lax.shift_right_logical(s_rel, bits(PLANE))
    s_block = (s_rel & (PLANE - 1)) * lines + (s_z ^ lax.shift_right_logical(s_z, 1))
    r_z = lax.shift_right_logical(r_patch, bits(PLANE)) ^ own_z
    r_block = (r_z ^ lax.shift_right_logical(r_z, 1)) + 1
    flags = jnp.where(lax.broadcasted_iota(I32, (8, count), 0) == member, 1.0, 0.0)
    before = jnp.where(
        lax.broadcasted_iota(I32, (count, count), 0) < lax.broadcasted_iota(I32, (count, count), 1),
        1.0,
        0.0,
    ).astype(BF)
    rank = jnp.sum(flags * mm(flags.astype(BF), before), axis=0, keepdims=True)
    pos = member * slot + rank.astype(I32)
    pos_ref[...] = pos
    row_at = lax.broadcasted_iota(I32, (8, count), 0)
    meta = jnp.where(row_at == 0, s_block, 0)
    meta = jnp.where(row_at == 1, s_within, meta)
    meta = jnp.where(row_at == 2, r_block, meta)
    meta = jnp.where(row_at == 3, r_within, meta).astype(F32).astype(BF)
    moved = match_columns(pos, PLANE * slot)
    placed = mm(moved, fe_ref[...]).astype(BF)
    for m, ref in enumerate(slot_refs):
        rows = slice(m * slot, (m + 1) * slot)
        ref[0:slot, :] = placed[rows]
        tail = lax.dot_general(
            meta, moved[rows], (((1,), (1,)), ((), ())), preferred_element_type=F32
        )
        ref[slot:, :] = jnp.zeros((ref.shape[0] - slot, ref.shape[1]), BF)
        ref[slot : slot + 16, 0:slot] = jnp.concatenate(
            [tail, jnp.zeros((8, slot), F32)], axis=0
        ).astype(BF)
    for copy in copies[3:]:
        copy.wait()


def load_kernel(picks, *refs):
    sources, held, sems = refs[: -len(picks) - 1], refs[-len(picks) - 1 : -1], refs[-1]
    copies = []
    for i, (which, layer) in enumerate(picks):
        source = sources[which] if layer is None else sources[which].at[layer]
        copies.append(pltpu.make_async_copy(source, held[i], sems.at[i]))
        copies[i].start()
    for copy in copies:
        copy.wait()


def edge_tail(pre_act, w_out, bias, gain, shift):
    hidden = silu(pre_act + bias).astype(BF)
    return layer_norm(mm(hidden, w_out), gain, shift)


def local_kernel(layer, rows, *refs):
    coarse_ref, rest_ref, edges_ref, send_ref, recv_ref, win_ref, wout_ref = refs[0:7]
    vec_refs, before, (new_ref, sum_ref) = refs[7:10], refs[10:-2], refs[-2:]
    nodes = jnp.concatenate([coarse_ref[...], rest_ref[...]], axis=0)
    node_count = nodes.shape[0]
    if before:
        new_ref[0 : rows.start, :] = before[0][0 : rows.start, :]
    total = before[1][...] if before else None
    block = min(rows.stop - rows.start, 512)
    for start in range(rows.start, rows.stop, block):
        send = send_ref[start : start + block].reshape(1, -1)
        recv = recv_ref[start : start + block].reshape(1, -1)
        edges = edges_ref[start : start + block, :]
        senders = mm(match_rows(as_column(send), node_count), nodes).astype(BF)
        receivers = mm(match_rows(as_column(recv), node_count), nodes).astype(BF)
        stacked = jnp.concatenate([edges, senders, receivers], axis=1)
        normed = edge_tail(
            mm(stacked, win_ref[...]), wout_ref[...], *[v[layer : layer + 1, :] for v in vec_refs]
        )
        new_ref[start : start + block, :] = (edges.astype(F32) + normed).astype(BF)
        part = mm(match_columns(recv, node_count), normed.astype(BF))
        total = part if total is None else total + part
    sum_ref[...] = total


def far_ready_kernel(lines, slot, *refs):
    slots, (table_ref, win_ref) = refs[0:PLANE], refs[PLANE : PLANE + 2]
    out_ref, early_ref, late_ref, scatter_ref = refs[PLANE + 2 :]
    span, width = lines * COARSE, table_ref.shape[1]
    columns_s, columns_r, rows_r = [], [], []
    for ref in slots:
        meta = ref[slot : slot + 16, :].astype(F32)[0:8, 0 : -(-slot // 128) * 128]
        tall = jnp.transpose(meta)[0:slot, :]
        columns_s.append((tall[:, 0:1] * COARSE + tall[:, 1:2]).astype(I32))
        columns_r.append((tall[:, 2:3] * COARSE + tall[:, 3:4]).astype(I32) - COARSE)
        rows_r.append((meta[2:3, 0:slot] * COARSE + meta[3:4, 0:slot]).astype(I32) - COARSE)
    column_s, column_r = jnp.concatenate(columns_s, axis=0), jnp.concatenate(columns_r, axis=0)
    receivers = mm(match_rows(column_r, span), table_ref[...]).astype(BF)
    edges = jnp.concatenate([ref[0:slot, :] for ref in slots], axis=0)
    product = mm(edges, win_ref[0:width, :])
    out_ref[...] = product + mm(receivers, win_ref[2 * width :, :])
    early_ref[...] = match_rows(column_s, 2 * span)
    late_ref[...] = match_rows(column_s, 2 * span, 2 * span)
    scatter_ref[...] = match_columns(jnp.concatenate(rows_r, axis=1), span)


def far_first_kernel(straight_ref, across_ref, pre_ref, early_ref, win_ref, out_ref):
    width = pre_ref.shape[1]
    table = jnp.concatenate([straight_ref[...], across_ref[...]], axis=0)
    senders = mm(early_ref[...], table).astype(BF)
    out_ref[...] = pre_ref[...] + mm(senders, win_ref[width : 2 * width, :])


def far_second_kernel(layer, lines, slot, start, chained, keep, *refs):
    straight_ref, across_ref, pre_ref, late_ref, scatter_ref, *refs = refs
    total, refs = (refs[0][...], refs[1:]) if chained else (None, refs)
    win_ref, wout_ref = refs[0:2]
    vecs, refs = [v[layer : layer + 1, :] for v in refs[2:5]], refs[5:]
    count = scatter_ref.shape[1] // slot
    slots, new_refs, sum_refs = refs[0:count], refs[count : 2 * count], refs[2 * count :]
    rows, width = slice(start * slot, (start + count) * slot), pre_ref.shape[1]
    table = jnp.concatenate([straight_ref[...], across_ref[...]], axis=0)
    senders = mm(late_ref[rows, :], table).astype(BF)
    pre_act = pre_ref[rows, :] + mm(senders, win_ref[width : 2 * width, :])
    normed = edge_tail(pre_act, wout_ref[...], *vecs)
    edges = jnp.concatenate([ref[0:slot, :] for ref in slots], axis=0)
    new = (edges.astype(F32) + normed).astype(BF)
    for j in range(count):
        new_refs[j][0:slot, :] = new[j * slot : (j + 1) * slot, :]
        if keep:
            new_refs[j][slot:, :] = slots[j][slot:, :]
    part = mm(scatter_ref[...], normed.astype(BF))
    total = part if total is None else total + part
    if len(sum_refs) == 1:
        sum_refs[0][...] = total
        return
    sum_refs[0][...] = total[0:COARSE, :]
    for i, ref in enumerate(sum_refs[1:]):
        ref[...] = total[(i + 1) * COARSE : (i + 2) * COARSE, :].astype(BF)


def node_tail(layer, nodes, pre_act, wout_ref, vec_refs):
    bias, gain, shift = [v[layer : layer + 1, :] for v in vec_refs]
    normed = edge_tail(pre_act, wout_ref[layer], bias, gain, shift)
    return (nodes.astype(F32) + normed).astype(BF)


def rest_kernel(layer, coarse_ref, nodes_ref, sum_ref, win_ref, wout_ref, *refs):
    nodes, width = nodes_ref[...], nodes_ref.shape[1]
    both = jnp.concatenate([coarse_ref[...], nodes], axis=0)
    pre_act = mm(both, win_ref[layer, 0:width, :])
    vec_refs, refs, coarse_pre_ref = refs[0:3], refs[3:-1], refs[-1]
    coarse_pre_ref[...] = pre_act[0:COARSE, :]
    sums = sum_ref[COARSE:, :].astype(BF)
    pre_act = pre_act[COARSE:, :] + mm(sums, win_ref[layer, width:, :])
    new = node_tail(layer, nodes, pre_act, wout_ref, vec_refs)
    if len(refs) == 1:
        refs[0][...] = new
        return
    pos_ref, *slot_refs, out_ref, half_ref, back_ref = refs
    out_ref[...] = new
    column, count = as_column(pos_ref[...]), back_ref.shape[1]
    slots = jnp.concatenate([ref[...] for ref in slot_refs], axis=0)
    half_ref[...] = mm(match_rows(column, count), slots).astype(BF)
    back_ref[...] = match_rows(column, count, count)


def coarse_kernel(layer, lines, nodes_ref, pre_ref, sum_ref, *refs):
    part_refs, refs = refs[0:lines], refs[lines:]
    (win_ref, wout_ref), vec_refs, refs = refs[0:2], refs[2:5], refs[5:]
    copies = []
    if len(refs) > 1:
        rest_ref, half_ref, back_ref, *slot_refs, out_hbm, far_hbm, out_ref, far_ref, sems = refs
        copies.append(pltpu.make_async_copy(rest_ref, out_hbm.at[COARSE:, :], sems.at[0]))
        copies[0].start()
        slots = jnp.concatenate([ref[...] for ref in slot_refs], axis=0)
        far_ref[...] = (half_ref[...].astype(F32) + mm(back_ref[...], slots)).astype(BF)
        copies.append(pltpu.make_async_copy(far_ref, far_hbm, sems.at[1]))
        copies[1].start()
    else:
        out_ref = refs[0]
    sums = sum_ref[0:COARSE, :] + part_refs[0][...]
    for ref in part_refs[1:]:
        sums = sums + ref[...].astype(F32)
    pre_act = pre_ref[...] + mm(sums.astype(BF), win_ref[layer, sums.shape[1] :, :])
    out_ref[...] = node_tail(layer, nodes_ref[...], pre_act, wout_ref, vec_refs)
    if copies:
        copies.append(pltpu.make_async_copy(out_ref, out_hbm.at[0:COARSE, :], sems.at[2]))
        copies[2].start()
        for copy in copies:
            copy.wait()


def call(kernel, outs, args, flops, limit, first=None, scratch=(), placed=pltpu.VMEM):
    bytes_accessed = sum(a.size * a.dtype.itemsize for a in [*args, *outs]) if flops or first == 0 else 0
    whole = pl.BlockSpec(memory_space=pltpu.VMEM)
    specs = [whole] * len(args)
    if first is not None:
        specs = [pl.BlockSpec(memory_space=pltpu.SMEM)] * first
        specs += [pl.BlockSpec(memory_space=pltpu.HBM)] * (len(args) - first)
        args = list(args[:first]) + [
            pltpu.with_memory_space_constraint(a, pltpu.HBM) for a in args[first:]
        ]
    return pl.pallas_call(
        kernel,
        out_shape=outs,
        in_specs=specs,
        out_specs=[pl.BlockSpec(memory_space=placed)] * len(outs),
        scratch_shapes=scratch,
        compiler_params=pltpu.CompilerParams(vmem_limit_bytes=limit),
        cost_estimate=pl.CostEstimate(flops=flops, bytes_accessed=bytes_accessed, transcendentals=0),
    )(*args)


def body(
    node_feat,
    local_edges,
    far_edges,
    local_send,
    local_recv,
    far_send,
    far_recv,
    edge_in,
    edge_out,
    node_in,
    node_out,
    edge_bias,
    edge_gain,
    edge_shift,
    node_bias,
    node_gain,
    node_shift,
):
    devices = lax.axis_size("patch")
    lines = devices // PLANE
    node_count, width = node_feat.shape
    far_count, local_count = far_edges.shape[0], local_edges.shape[0]
    slot = lines * (5 * far_count // (2 * devices))
    padded = -(-(slot + 4) // 16) * 16
    layers = edge_in.shape[0]
    limit = (24 if lines <= 4 else 56) * 2**20
    shape = jax.ShapeDtypeStruct
    place = [0] * lines
    for z in range(lines):
        place[z ^ (z >> 1)] = z

    def swap(values, distance):
        return lax.ppermute(values, "patch", [(i, i ^ distance) for i in range(devices)])

    own = lax.axis_index("patch").reshape(1).astype(I32)
    fs, fr = far_send.reshape(1, -1), far_recv.reshape(1, -1)
    tied = lax.optimization_barrier
    prepared = call(
        functools.partial(prep_kernel, node_count, lines, slot),
        [shape((1, far_count), I32), shape((COARSE, width), BF)]
        + [shape((node_count - COARSE, width), BF)]
        + [shape((padded, width), BF)] * PLANE,
        [own, fs, fr, far_edges, node_feat],
        2 * PLANE * slot * far_count * width,
        limit,
        first=1,
        scratch=[
            pltpu.VMEM((1, far_count), I32),
            pltpu.VMEM((1, far_count), I32),
            pltpu.VMEM((far_count, width), BF),
            pltpu.SemaphoreType.DMA((5,)),
        ],
    )
    pos, coarse, rest, slots = *prepared[0:3], prepared[3:]
    slots = [slots[0]] + [swap(slots[m], m) for m in range(1, PLANE)]
    def fetch(sources, picks):
        pieces = [sources[i] if layer is None else sources[i][0] for i, layer in picks]
        return call(
            functools.partial(load_kernel, picks),
            [shape(v.shape, v.dtype) for v in pieces],
            sources,
            0,
            limit,
            first=0,
            scratch=[pltpu.SemaphoreType.DMA((len(picks),))],
        )

    first = [local_edges, local_send, local_recv, edge_bias, edge_gain, edge_shift]
    picks = [(i, None) for i in range(len(first))] + [(len(first), 0), (len(first) + 1, 0)]
    first = fetch([*first, edge_in, edge_out], picks)
    far_rows, span = PLANE * slot, lines * COARSE
    cut = local_count // 3 * 2 // 256 * 256
    pieces = [slice(0, cut), slice(cut, local_count)] if cut else [slice(0, local_count)]
    local, local_send, local_recv = first[0:3]
    edge_vecs, weights = first[3:6], [first[6:8]]
    for l in range(layers):
        last = l == layers - 1

        def local_part(rows, before=(), share=1):
            return call(
                functools.partial(local_kernel, l, rows),
                [shape((rows.stop, width), BF), shape((node_count, width), F32)],
                [coarse, rest, local, local_send, local_recv, *weights[l], *edge_vecs, *before],
                2 * (rows.stop - rows.start) * width * (3 * node_count + 4 * width) * share,
                limit,
            )

        done = local_part(pieces[0], share=min(l, 1))
        if lines == 4:
            z3, z1 = swap(coarse, 12), swap(coarse, 4)
            if l:
                z3, z1, done = tied((z3, z1, done))
            else:
                z3, z1, done, slots = tied((z3, z1, done, slots))
            near = jnp.concatenate([coarse, z1, z3], axis=0)
            z2 = swap(z3, 4)
            across = swap(near, 2)
        else:
            near = [coarse if z == 0 else swap(coarse, PLANE * z) for z in place]
            near, z2 = jnp.concatenate(near[:-1], axis=0), near[-1]
            across = swap(near, 2)
        if not last:
            z2, done = tied((z2, done))
            for rows in pieces[1:]:
                done = local_part(rows, done)
        late = swap(z2, 2)
        table = jnp.concatenate([near, z2], axis=0)
        tables = [table, swap(table, 1)]
        pre_act, early, *found = call(
            functools.partial(far_ready_kernel, lines, slot),
            [shape((far_rows, width), F32)]
            + [shape((far_rows, 2 * span), BF)] * 2
            + [shape((span, far_rows), BF)],
            [*slots, table, weights[l][0]],
            2 * far_rows * width * (span + 2 * width),
            limit,
        )
        pre_act = call(
            far_first_kernel,
            [shape((far_rows, width), F32)],
            [*tables, pre_act, early, weights[l][0]],
            2 * far_rows * width * (2 * span + width),
            limit,
        )
        found = [*pre_act, *found]
        late, found, done = tied((late, found, done))
        late = jnp.concatenate([across, late], axis=0)
        late = [late, swap(late, 1)]
        moved = shape((slot if last else padded, width), BF)
        parts_shape = [shape((COARSE, width), F32)] + [shape((COARSE, width), BF)] * (lines - 1)

        def far_part(start, size, before, outs):
            return call(
                functools.partial(far_second_kernel, l, lines, slot, start, len(before) > 0, not last),
                [moved] * size + outs,
                [*late, *found[0:2], found[2 + start // size], *before]
                + [*weights[l], *edge_vecs, *slots[start : start + size]],
                2 * size * slot * width * (3 * span + 2 * width),
                limit,
            )

        far = far_part(0, PLANE, [], parts_shape)
        slots, parts = [*far[:PLANE]], far[PLANE:]
        if last:
            slots = [slots[0]] + [swap(slots[m], m) for m in range(1, PLANE)]
            parts, done = tied((parts, done))
            for rows in pieces[1:]:
                done = local_part(rows, done)
        local, sums = done
        far_parts = [swap(parts[i], PLANE * place[i]) for i in range(lines - 1, 0, -1)]
        parts = [parts[0], *far_parts]
        if l == 0:
            sources = [node_in, node_out, node_bias, node_gain, node_shift]
            picks = [(i, None) for i in range(len(sources))]
            for i in range(1, layers):
                picks += [(len(sources), i), (len(sources) + 1, i)]
            sources, sums = tied(([*sources, edge_in, edge_out], sums))
            second = fetch(sources, picks)
            node_in, node_out, node_vecs = *second[0:2], second[2:5]
            weights += [second[5 + 2 * i : 7 + 2 * i] for i in range(layers - 1)]
        ends = [node_in, node_out, *node_vecs]
        *rest, coarse_pre = call(
            functools.partial(rest_kernel, l),
            [shape((node_count - COARSE, width), BF)]
            + [shape((far_count, width), BF), shape((far_count, 2 * slot), BF)] * last
            + [shape((COARSE, width), F32)],
            [coarse, rest, sums, *ends] + [pos, *slots[0:2]] * last,
            6 * (node_count - COARSE) * width * width,
            limit,
        )
        if last:
            return_shapes = [shape((node_count, width), BF), shape((far_count, width), BF)]
            extra = [*rest, *slots[2:]]
            scratch = [pltpu.VMEM((COARSE, width), BF), pltpu.VMEM((far_count, width), BF)]
            scratch += [pltpu.SemaphoreType.DMA((3,))]
        else:
            return_shapes, extra, rest = [shape((COARSE, width), BF)], [], rest[0]
        coarse, *far_out = call(
            functools.partial(coarse_kernel, l, lines),
            return_shapes,
            [coarse, coarse_pre, sums, *parts, *ends, *extra],
            6 * COARSE * width * width,
            limit,
            scratch=scratch if last else (),
            placed=pltpu.HBM if last else pltpu.VMEM,
        )
    return (coarse, local, far_out[0])


def solution(mesh):
    split = P(("groups", "patch"), None)
    line = P(("groups", "patch"))
    return jax.shard_map(
        body,
        mesh=mesh,
        in_specs=(split,) * 3 + (line,) * 4 + (P(),) * 10,
        out_specs=(split,) * 3,
        check_vma=False,
    )
```

```python
import functools

import jax
import jax.numpy as jnp
from jax import lax
from jax.experimental import pallas as pl
from jax.experimental.pallas import tpu as pltpu
from jax.sharding import PartitionSpec as P

COARSE = 64
PLANE = 4
BF = jnp.bfloat16
F32 = jnp.float32
I32 = jnp.int32


def mm(left, right):
    return jnp.dot(left, right, preferred_element_type=F32)


def silu(values):
    half = 0.5 * values
    return half * jnp.tanh(half) + half


def layer_norm(values, gain, shift):
    mean_value = jnp.mean(values, axis=-1, keepdims=True)
    centred = values - mean_value
    variance = jnp.mean(centred * centred, axis=-1, keepdims=True)
    return centred * lax.rsqrt(variance + 1e-05) * gain + shift


def match_rows(column, count, offset=0):
    where = lax.broadcasted_iota(I32, (column.shape[0], count), 1) + offset
    return jnp.where(where == column, 1.0, 0.0).astype(BF)


def match_columns(row, count, offset=0):
    where = lax.broadcasted_iota(I32, (count, row.shape[1]), 0) + offset
    return jnp.where(where == row, 1.0, 0.0).astype(BF)


def as_column(row):
    tall = jnp.broadcast_to(row.astype(F32), (8, row.shape[1]))
    return jnp.transpose(tall)[:, :1].astype(I32)


def bits(count):
    assert count & (count - 1) == 0
    return count.bit_length() - 1


def prep_kernel(node_count, lines, slot, own_ref, fs_hbm, fr_hbm, fe_hbm, nodes_hbm, *refs):
    pos_ref, coarse_ref, rest_ref, slot_refs = *refs[0:3], refs[3 : 3 + PLANE]
    fs_ref, fr_ref, fe_ref, sems = refs[3 + PLANE :]
    moves = [
        (fs_hbm, fs_ref),
        (fr_hbm, fr_ref),
        (fe_hbm, fe_ref),
        (nodes_hbm.at[0:COARSE, :], coarse_ref),
        (nodes_hbm.at[COARSE:, :], rest_ref),
    ]
    copies = [pltpu.make_async_copy(a, b, sems.at[i]) for i, (a, b) in enumerate(moves)]
    for copy in copies:
        copy.start()
    for copy in copies[0:3]:
        copy.wait()
    own = own_ref[0]
    own_q, own_z = own & (PLANE - 1), lax.shift_right_logical(own, bits(PLANE))
    fs, fr = fs_ref[...], fr_ref[...]
    count = fs.shape[1]
    shift = bits(node_count)
    s_patch, s_within = lax.shift_right_logical(fs, shift), fs & (node_count - 1)
    r_patch, r_within = lax.shift_right_logical(fr, shift), fr & (node_count - 1)
    r_q = r_patch & (PLANE - 1)
    member = r_q ^ own_q
    s_rel = s_patch ^ (own_z * PLANE + r_q)
    s_z = lax.shift_right_logical(s_rel, bits(PLANE))
    s_block = (s_rel & (PLANE - 1)) * lines + s_z
    r_z = lax.shift_right_logical(r_patch, bits(PLANE)) ^ own_z
    r_block = r_z + 1
    flags = jnp.where(lax.broadcasted_iota(I32, (8, count), 0) == member, 1.0, 0.0)
    before = jnp.where(
        lax.broadcasted_iota(I32, (count, count), 0) < lax.broadcasted_iota(I32, (count, count), 1),
        1.0,
        0.0,
    ).astype(BF)
    rank = jnp.sum(flags * mm(flags.astype(BF), before), axis=0, keepdims=True)
    pos = member * slot + rank.astype(I32)
    pos_ref[...] = pos
    row_at = lax.broadcasted_iota(I32, (8, count), 0)
    meta = jnp.where(row_at == 0, s_block, 0)
    meta = jnp.where(row_at == 1, s_within, meta)
    meta = jnp.where(row_at == 2, r_block, meta)
    meta = jnp.where(row_at == 3, r_within, meta).astype(F32).astype(BF)
    moved = match_columns(pos, PLANE * slot)
    placed = mm(moved, fe_ref[...]).astype(BF)
    for m, ref in enumerate(slot_refs):
        rows = slice(m * slot, (m + 1) * slot)
        ref[0:slot, :] = placed[rows]
        tail = lax.dot_general(
            meta, moved[rows], (((1,), (1,)), ((), ())), preferred_element_type=F32
        )
        ref[slot:, :] = jnp.zeros((ref.shape[0] - slot, ref.shape[1]), BF)
        ref[slot : slot + 16, 0:slot] = jnp.concatenate(
            [tail, jnp.zeros((8, slot), F32)], axis=0
        ).astype(BF)
    for copy in copies[3:]:
        copy.wait()


def load_kernel(picks, *refs):
    sources, held, sems = refs[: -len(picks) - 1], refs[-len(picks) - 1 : -1], refs[-1]
    copies = []
    for i, (which, layer) in enumerate(picks):
        source = sources[which] if layer is None else sources[which].at[layer]
        copies.append(pltpu.make_async_copy(source, held[i], sems.at[i]))
        copies[i].start()
    for copy in copies:
        copy.wait()


def edge_tail(pre_act, w_out, bias, gain, shift):
    hidden = silu(pre_act + bias).astype(BF)
    return layer_norm(mm(hidden, w_out), gain, shift)


def local_kernel(layer, rows, *refs):
    coarse_ref, rest_ref, edges_ref, send_ref, recv_ref, win_ref, wout_ref = refs[0:7]
    vec_refs, before, (new_ref, sum_ref) = refs[7:10], refs[10:-2], refs[-2:]
    nodes = jnp.concatenate([coarse_ref[...], rest_ref[...]], axis=0)
    node_count = nodes.shape[0]
    if before:
        new_ref[0 : rows.start, :] = before[0][0 : rows.start, :]
    total = before[1][...] if before else None
    block = min(rows.stop - rows.start, 512)
    for start in range(rows.start, rows.stop, block):
        send = send_ref[start : start + block].reshape(1, -1)
        recv = recv_ref[start : start + block].reshape(1, -1)
        edges = edges_ref[start : start + block, :]
        senders = mm(match_rows(as_column(send), node_count), nodes).astype(BF)
        receivers = mm(match_rows(as_column(recv), node_count), nodes).astype(BF)
        stacked = jnp.concatenate([edges, senders, receivers], axis=1)
        normed = edge_tail(
            mm(stacked, win_ref[...]), wout_ref[...], *[v[layer : layer + 1, :] for v in vec_refs]
        )
        new_ref[start : start + block, :] = (edges.astype(F32) + normed).astype(BF)
        part = mm(match_columns(recv, node_count), normed.astype(BF))
        total = part if total is None else total + part
    sum_ref[...] = total


def far_ready_kernel(lines, slot, *refs):
    slots, (table_ref, win_ref) = refs[0:PLANE], refs[PLANE : PLANE + 2]
    out_ref, early_ref, late_ref, scatter_ref = refs[PLANE + 2 :]
    span, width = lines * COARSE, table_ref.shape[1]
    columns_s, columns_r, rows_r = [], [], []
    for ref in slots:
        meta = ref[slot : slot + 16, :].astype(F32)[0:8, 0 : -(-slot // 128) * 128]
        tall = jnp.transpose(meta)[0:slot, :]
        columns_s.append((tall[:, 0:1] * COARSE + tall[:, 1:2]).astype(I32))
        columns_r.append((tall[:, 2:3] * COARSE + tall[:, 3:4]).astype(I32) - COARSE)
        rows_r.append((meta[2:3, 0:slot] * COARSE + meta[3:4, 0:slot]).astype(I32) - COARSE)
    column_s, column_r = jnp.concatenate(columns_s, axis=0), jnp.concatenate(columns_r, axis=0)
    receivers = mm(match_rows(column_r, span), table_ref[...]).astype(BF)
    edges = jnp.concatenate([ref[0:slot, :] for ref in slots], axis=0)
    product = mm(edges, win_ref[0:width, :])
    out_ref[...] = product + mm(receivers, win_ref[2 * width :, :])
    early_ref[...] = match_rows(column_s, 2 * span)
    late_ref[...] = match_rows(column_s, 2 * span, 2 * span)
    scatter_ref[...] = match_columns(jnp.concatenate(rows_r, axis=1), span)


def far_first_kernel(straight_ref, across_ref, pre_ref, early_ref, win_ref, out_ref):
    width = pre_ref.shape[1]
    table = jnp.concatenate([straight_ref[...], across_ref[...]], axis=0)
    senders = mm(early_ref[...], table).astype(BF)
    out_ref[...] = pre_ref[...] + mm(senders, win_ref[width : 2 * width, :])


def far_second_kernel(layer, lines, slot, start, chained, keep, *refs):
    straight_ref, across_ref, pre_ref, late_ref, scatter_ref, *refs = refs
    total, refs = (refs[0][...], refs[1:]) if chained else (None, refs)
    win_ref, wout_ref = refs[0:2]
    vecs, refs = [v[layer : layer + 1, :] for v in refs[2:5]], refs[5:]
    count = scatter_ref.shape[1] // slot
    slots, new_refs, sum_refs = refs[0:count], refs[count : 2 * count], refs[2 * count :]
    rows, width = slice(start * slot, (start + count) * slot), pre_ref.shape[1]
    table = jnp.concatenate([straight_ref[...], across_ref[...]], axis=0)
    senders = mm(late_ref[rows, :], table).astype(BF)
    pre_act = pre_ref[rows, :] + mm(senders, win_ref[width : 2 * width, :])
    normed = edge_tail(pre_act, wout_ref[...], *vecs)
    edges = jnp.concatenate([ref[0:slot, :] for ref in slots], axis=0)
    new = (edges.astype(F32) + normed).astype(BF)
    for j in range(count):
        new_refs[j][0:slot, :] = new[j * slot : (j + 1) * slot, :]
        if keep:
            new_refs[j][slot:, :] = slots[j][slot:, :]
    part = mm(scatter_ref[...], normed.astype(BF))
    total = part if total is None else total + part
    if len(sum_refs) == 1:
        sum_refs[0][...] = total
        return
    sum_refs[0][...] = total[0:COARSE, :]
    for i, ref in enumerate(sum_refs[1:]):
        ref[...] = total[(i + 1) * COARSE : (i + 2) * COARSE, :].astype(BF)


def node_tail(layer, nodes, pre_act, wout_ref, vec_refs):
    bias, gain, shift = [v[layer : layer + 1, :] for v in vec_refs]
    normed = edge_tail(pre_act, wout_ref[layer], bias, gain, shift)
    return (nodes.astype(F32) + normed).astype(BF)


def rest_kernel(layer, coarse_ref, nodes_ref, sum_ref, win_ref, wout_ref, *refs):
    nodes, width = nodes_ref[...], nodes_ref.shape[1]
    both = jnp.concatenate([coarse_ref[...], nodes], axis=0)
    pre_act = mm(both, win_ref[layer, 0:width, :])
    vec_refs, refs, coarse_pre_ref = refs[0:3], refs[3:-1], refs[-1]
    coarse_pre_ref[...] = pre_act[0:COARSE, :]
    sums = sum_ref[COARSE:, :].astype(BF)
    pre_act = pre_act[COARSE:, :] + mm(sums, win_ref[layer, width:, :])
    new = node_tail(layer, nodes, pre_act, wout_ref, vec_refs)
    if len(refs) == 1:
        refs[0][...] = new
        return
    pos_ref, *slot_refs, out_ref, half_ref, back_ref = refs
    out_ref[...] = new
    column, count = as_column(pos_ref[...]), back_ref.shape[1]
    slots = jnp.concatenate([ref[...] for ref in slot_refs], axis=0)
    half_ref[...] = mm(match_rows(column, count), slots).astype(BF)
    back_ref[...] = match_rows(column, count, count)


def coarse_kernel(layer, lines, nodes_ref, pre_ref, sum_ref, *refs):
    part_refs, refs = refs[0:lines], refs[lines:]
    (win_ref, wout_ref), vec_refs, refs = refs[0:2], refs[2:5], refs[5:]
    copies = []
    if len(refs) > 1:
        rest_ref, half_ref, back_ref, *slot_refs, out_hbm, far_hbm, out_ref, far_ref, sems = refs
        copies.append(pltpu.make_async_copy(rest_ref, out_hbm.at[COARSE:, :], sems.at[0]))
        copies[0].start()
        slots = jnp.concatenate([ref[...] for ref in slot_refs], axis=0)
        far_ref[...] = (half_ref[...].astype(F32) + mm(back_ref[...], slots)).astype(BF)
        copies.append(pltpu.make_async_copy(far_ref, far_hbm, sems.at[1]))
        copies[1].start()
    else:
        out_ref = refs[0]
    sums = sum_ref[0:COARSE, :] + part_refs[0][...]
    for ref in part_refs[1:]:
        sums = sums + ref[...].astype(F32)
    pre_act = pre_ref[...] + mm(sums.astype(BF), win_ref[layer, sums.shape[1] :, :])
    out_ref[...] = node_tail(layer, nodes_ref[...], pre_act, wout_ref, vec_refs)
    if copies:
        copies.append(pltpu.make_async_copy(out_ref, out_hbm.at[0:COARSE, :], sems.at[2]))
        copies[2].start()
        for copy in copies:
            copy.wait()


def call(kernel, outs, args, flops, limit, first=None, scratch=(), placed=pltpu.VMEM):
    bytes_accessed = sum(a.size * a.dtype.itemsize for a in [*args, *outs]) if flops or first == 0 else 0
    whole = pl.BlockSpec(memory_space=pltpu.VMEM)
    specs = [whole] * len(args)
    if first is not None:
        specs = [pl.BlockSpec(memory_space=pltpu.SMEM)] * first
        specs += [pl.BlockSpec(memory_space=pltpu.HBM)] * (len(args) - first)
        args = list(args[:first]) + [
            pltpu.with_memory_space_constraint(a, pltpu.HBM) for a in args[first:]
        ]
    return pl.pallas_call(
        kernel,
        out_shape=outs,
        in_specs=specs,
        out_specs=[pl.BlockSpec(memory_space=placed)] * len(outs),
        scratch_shapes=scratch,
        compiler_params=pltpu.CompilerParams(vmem_limit_bytes=limit),
        cost_estimate=pl.CostEstimate(flops=flops, bytes_accessed=bytes_accessed, transcendentals=0),
    )(*args)


def body(
    node_feat,
    local_edges,
    far_edges,
    local_send,
    local_recv,
    far_send,
    far_recv,
    edge_in,
    edge_out,
    node_in,
    node_out,
    edge_bias,
    edge_gain,
    edge_shift,
    node_bias,
    node_gain,
    node_shift,
):
    devices = lax.axis_size("patch")
    lines = devices // PLANE
    node_count, width = node_feat.shape
    far_count, local_count = far_edges.shape[0], local_edges.shape[0]
    slot = lines * (5 * far_count // (2 * devices))
    padded = -(-(slot + 4) // 16) * 16
    layers = edge_in.shape[0]
    limit = (24 if lines <= 4 else 56) * 2**20
    shape = jax.ShapeDtypeStruct

    def swap(values, distance):
        return lax.ppermute(values, "patch", [(i, i ^ distance) for i in range(devices)])

    own = lax.axis_index("patch").reshape(1).astype(I32)
    fs, fr = far_send.reshape(1, -1), far_recv.reshape(1, -1)
    tied = lax.optimization_barrier
    prepared = call(
        functools.partial(prep_kernel, node_count, lines, slot),
        [shape((1, far_count), I32), shape((COARSE, width), BF)]
        + [shape((node_count - COARSE, width), BF)]
        + [shape((padded, width), BF)] * PLANE,
        [own, fs, fr, far_edges, node_feat],
        2 * PLANE * slot * far_count * width,
        limit,
        first=1,
        scratch=[
            pltpu.VMEM((1, far_count), I32),
            pltpu.VMEM((1, far_count), I32),
            pltpu.VMEM((far_count, width), BF),
            pltpu.SemaphoreType.DMA((5,)),
        ],
    )
    pos, coarse, rest, slots = *prepared[0:3], prepared[3:]
    slots = [slots[0]] + [swap(slots[m], m) for m in range(1, PLANE)]
    def fetch(sources, picks):
        pieces = [sources[i] if layer is None else sources[i][0] for i, layer in picks]
        return call(
            functools.partial(load_kernel, picks),
            [shape(v.shape, v.dtype) for v in pieces],
            sources,
            0,
            limit,
            first=0,
            scratch=[pltpu.SemaphoreType.DMA((len(picks),))],
        )

    first = [local_edges, local_send, local_recv, edge_bias, edge_gain, edge_shift]
    picks = [(i, None) for i in range(len(first))] + [(len(first), 0), (len(first) + 1, 0)]
    first = fetch([*first, edge_in, edge_out], picks)
    far_rows, span = PLANE * slot, lines * COARSE
    cut = local_count // 3 * 2 // 256 * 256
    pieces = [slice(0, cut), slice(cut, local_count)] if cut else [slice(0, local_count)]
    local, local_send, local_recv = first[0:3]
    edge_vecs, weights = first[3:6], [first[6:8]]
    for l in range(layers):
        last = l == layers - 1

        def local_part(rows, before=(), share=1):
            return call(
                functools.partial(local_kernel, l, rows),
                [shape((rows.stop, width), BF), shape((node_count, width), F32)],
                [coarse, rest, local, local_send, local_recv, *weights[l], *edge_vecs, *before],
                2 * (rows.stop - rows.start) * width * (3 * node_count + 4 * width) * share,
                limit,
            )

        done = local_part(pieces[0], share=min(l, 1))
        if lines == 4:
            z2, z1 = swap(coarse, 8), swap(coarse, 4)
            if l:
                z2, z1, done = tied((z2, z1, done))
            else:
                z2, z1, done, slots = tied((z2, z1, done, slots))
            near = jnp.concatenate([coarse, z1, z2], axis=0)
            far_end = swap(z2, 4)
            across = swap(near, 2)
        else:
            near = [coarse] + [swap(coarse, PLANE * z) for z in range(1, lines)]
            near, far_end = jnp.concatenate(near[:-1], axis=0), near[-1]
            across = swap(near, 2)
        if not last:
            far_end, done = tied((far_end, done))
            for rows in pieces[1:]:
                done = local_part(rows, done)
        late = swap(far_end, 2)
        table = jnp.concatenate([near, far_end], axis=0)
        tables = [table, swap(table, 1)]
        pre_act, early, *found = call(
            functools.partial(far_ready_kernel, lines, slot),
            [shape((far_rows, width), F32)]
            + [shape((far_rows, 2 * span), BF)] * 2
            + [shape((span, far_rows), BF)],
            [*slots, table, weights[l][0]],
            2 * far_rows * width * (span + 2 * width),
            limit,
        )
        pre_act = call(
            far_first_kernel,
            [shape((far_rows, width), F32)],
            [*tables, pre_act, early, weights[l][0]],
            2 * far_rows * width * (2 * span + width),
            limit,
        )
        found = [*pre_act, *found]
        late, found, done = tied((late, found, done))
        late = jnp.concatenate([across, late], axis=0)
        late = [late, swap(late, 1)]
        moved = shape((slot if last else padded, width), BF)
        parts_shape = [shape((COARSE, width), F32)] + [shape((COARSE, width), BF)] * (lines - 1)

        def far_part(start, size, before, outs):
            return call(
                functools.partial(far_second_kernel, l, lines, slot, start, len(before) > 0, not last),
                [moved] * size + outs,
                [*late, *found[0:2], found[2 + start // size], *before]
                + [*weights[l], *edge_vecs, *slots[start : start + size]],
                2 * size * slot * width * (3 * span + 2 * width),
                limit,
            )

        far = far_part(0, PLANE, [], parts_shape)
        slots, parts = [*far[:PLANE]], far[PLANE:]
        if last:
            slots = [slots[0]] + [swap(slots[m], m) for m in range(1, PLANE)]
            parts, done = tied((parts, done))
            for rows in pieces[1:]:
                done = local_part(rows, done)
        local, sums = done
        far_parts = [swap(parts[z], PLANE * z) for z in [*range(2, lines), 1]]
        parts = [parts[0], *far_parts]
        if l == 0:
            sources = [node_in, node_out, node_bias, node_gain, node_shift]
            picks = [(i, None) for i in range(len(sources))]
            for i in range(1, layers):
                picks += [(len(sources), i), (len(sources) + 1, i)]
            sources, sums = tied(([*sources, edge_in, edge_out], sums))
            second = fetch(sources, picks)
            node_in, node_out, node_vecs = *second[0:2], second[2:5]
            weights += [second[5 + 2 * i : 7 + 2 * i] for i in range(layers - 1)]
        ends = [node_in, node_out, *node_vecs]
        *rest, coarse_pre = call(
            functools.partial(rest_kernel, l),
            [shape((node_count - COARSE, width), BF)]
            + [shape((far_count, width), BF), shape((far_count, 2 * slot), BF)] * last
            + [shape((COARSE, width), F32)],
            [coarse, rest, sums, *ends] + [pos, *slots[0:2]] * last,
            6 * (node_count - COARSE) * width * width,
            limit,
        )
        if last:
            return_shapes = [shape((node_count, width), BF), shape((far_count, width), BF)]
            extra = [*rest, *slots[2:]]
            scratch = [pltpu.VMEM((COARSE, width), BF), pltpu.VMEM((far_count, width), BF)]
            scratch += [pltpu.SemaphoreType.DMA((3,))]
        else:
            return_shapes, extra, rest = [shape((COARSE, width), BF)], [], rest[0]
        coarse, *far_out = call(
            functools.partial(coarse_kernel, l, lines),
            return_shapes,
            [coarse, coarse_pre, sums, *parts, *ends, *extra],
            6 * COARSE * width * width,
            limit,
            scratch=scratch if last else (),
            placed=pltpu.HBM if last else pltpu.VMEM,
        )
    return (coarse, local, far_out[0])


def solution(mesh):
    split = P(("groups", "patch"), None)
    line = P(("groups", "patch"))
    return jax.shard_map(
        body,
        mesh=mesh,
        in_specs=(split,) * 3 + (line,) * 4 + (P(),) * 10,
        out_specs=(split,) * 3,
        check_vma=False,
    )
```

```python
import functools

import jax
import jax.numpy as jnp
from jax import lax
from jax.experimental import pallas as pl
from jax.experimental.pallas import tpu as pltpu
from jax.sharding import PartitionSpec as P

COARSE = 64
PLANE = 4
BF = jnp.bfloat16
F32 = jnp.float32
I32 = jnp.int32


def mm(left, right):
    return jnp.dot(left, right, preferred_element_type=F32)


def silu(values):
    half = 0.5 * values
    return half * jnp.tanh(half) + half


def layer_norm(values, gain, shift):
    mean_value = jnp.mean(values, axis=-1, keepdims=True)
    centred = values - mean_value
    variance = jnp.mean(centred * centred, axis=-1, keepdims=True)
    return centred * lax.rsqrt(variance + 1e-05) * gain + shift


def match_rows(column, count, offset=0):
    where = lax.broadcasted_iota(I32, (column.shape[0], count), 1) + offset
    return jnp.where(where == column, 1.0, 0.0).astype(BF)


def match_columns(row, count, offset=0):
    where = lax.broadcasted_iota(I32, (count, row.shape[1]), 0) + offset
    return jnp.where(where == row, 1.0, 0.0).astype(BF)


def as_column(row):
    tall = jnp.broadcast_to(row.astype(F32), (8, row.shape[1]))
    return jnp.transpose(tall)[:, :1].astype(I32)


def bits(count):
    assert count & (count - 1) == 0
    return count.bit_length() - 1


def prep_kernel(node_count, lines, slot, own_ref, fs_hbm, fr_hbm, fe_hbm, nodes_hbm, *refs):
    pos_ref, coarse_ref, rest_ref, slot_refs = *refs[0:3], refs[3 : 3 + PLANE]
    fs_ref, fr_ref, fe_ref, sems = refs[3 + PLANE :]
    moves = [
        (fs_hbm, fs_ref),
        (fr_hbm, fr_ref),
        (fe_hbm, fe_ref),
        (nodes_hbm.at[0:COARSE, :], coarse_ref),
        (nodes_hbm.at[COARSE:, :], rest_ref),
    ]
    copies = [pltpu.make_async_copy(a, b, sems.at[i]) for i, (a, b) in enumerate(moves)]
    for copy in copies:
        copy.start()
    for copy in copies[0:3]:
        copy.wait()
    own = own_ref[0]
    own_q, own_z = own & (PLANE - 1), lax.shift_right_logical(own, bits(PLANE))
    fs, fr = fs_ref[...], fr_ref[...]
    count = fs.shape[1]
    shift = bits(node_count)
    s_patch, s_within = lax.shift_right_logical(fs, shift), fs & (node_count - 1)
    r_patch, r_within = lax.shift_right_logical(fr, shift), fr & (node_count - 1)
    r_q = r_patch & (PLANE - 1)
    member = r_q ^ own_q
    s_rel = s_patch ^ (own_z * PLANE + r_q)
    s_z = lax.shift_right_logical(s_rel, bits(PLANE))
    s_block = (s_rel & (PLANE - 1)) * lines + s_z
    r_z = lax.shift_right_logical(r_patch, bits(PLANE)) ^ own_z
    r_block = r_z + 1
    flags = jnp.where(lax.broadcasted_iota(I32, (8, count), 0) == member, 1.0, 0.0)
    before = jnp.where(
        lax.broadcasted_iota(I32, (count, count), 0) < lax.broadcasted_iota(I32, (count, count), 1),
        1.0,
        0.0,
    ).astype(BF)
    rank = jnp.sum(flags * mm(flags.astype(BF), before), axis=0, keepdims=True)
    pos = member * slot + rank.astype(I32)
    pos_ref[...] = pos
    row_at = lax.broadcasted_iota(I32, (8, count), 0)
    meta = jnp.where(row_at == 0, s_block, 0)
    meta = jnp.where(row_at == 1, s_within, meta)
    meta = jnp.where(row_at == 2, r_block, meta)
    meta = jnp.where(row_at == 3, r_within, meta).astype(F32).astype(BF)
    moved = match_columns(pos, PLANE * slot)
    placed = mm(moved, fe_ref[...]).astype(BF)
    for m, ref in enumerate(slot_refs):
        rows = slice(m * slot, (m + 1) * slot)
        ref[0:slot, :] = placed[rows]
        tail = lax.dot_general(
            meta, moved[rows], (((1,), (1,)), ((), ())), preferred_element_type=F32
        )
        ref[slot:, :] = jnp.zeros((ref.shape[0] - slot, ref.shape[1]), BF)
        ref[slot : slot + 16, 0:slot] = jnp.concatenate(
            [tail, jnp.zeros((8, slot), F32)], axis=0
        ).astype(BF)
    for copy in copies[3:]:
        copy.wait()


def load_kernel(picks, *refs):
    sources, held, sems = refs[: -len(picks) - 1], refs[-len(picks) - 1 : -1], refs[-1]
    copies = []
    for i, (which, layer) in enumerate(picks):
        source = sources[which] if layer is None else sources[which].at[layer]
        copies.append(pltpu.make_async_copy(source, held[i], sems.at[i]))
        copies[i].start()
    for copy in copies:
        copy.wait()


def edge_tail(pre_act, w_out, bias, gain, shift):
    hidden = silu(pre_act + bias).astype(BF)
    return layer_norm(mm(hidden, w_out), gain, shift)


def local_kernel(layer, rows, *refs):
    coarse_ref, rest_ref, edges_ref, send_ref, recv_ref, win_ref, wout_ref = refs[0:7]
    vec_refs, before, (new_ref, sum_ref) = refs[7:10], refs[10:-2], refs[-2:]
    nodes = jnp.concatenate([coarse_ref[...], rest_ref[...]], axis=0)
    node_count = nodes.shape[0]
    if before:
        new_ref[0 : rows.start, :] = before[0][0 : rows.start, :]
    total = before[1][...] if before else None
    block = min(rows.stop - rows.start, 512)
    for start in range(rows.start, rows.stop, block):
        send = send_ref[start : start + block].reshape(1, -1)
        recv = recv_ref[start : start + block].reshape(1, -1)
        edges = edges_ref[start : start + block, :]
        senders = mm(match_rows(as_column(send), node_count), nodes).astype(BF)
        receivers = mm(match_rows(as_column(recv), node_count), nodes).astype(BF)
        stacked = jnp.concatenate([edges, senders, receivers], axis=1)
        normed = edge_tail(
            mm(stacked, win_ref[...]), wout_ref[...], *[v[layer : layer + 1, :] for v in vec_refs]
        )
        new_ref[start : start + block, :] = (edges.astype(F32) + normed).astype(BF)
        part = mm(match_columns(recv, node_count), normed.astype(BF))
        total = part if total is None else total + part
    sum_ref[...] = total


def far_ready_kernel(lines, slot, *refs):
    slots, (table_ref, win_ref) = refs[0:PLANE], refs[PLANE : PLANE + 2]
    out_ref, early_ref, late_ref, scatter_ref = refs[PLANE + 2 :]
    span, width = lines * COARSE, table_ref.shape[1]
    columns_s, columns_r, rows_r = [], [], []
    for ref in slots:
        meta = ref[slot : slot + 16, :].astype(F32)[0:8, 0 : -(-slot // 128) * 128]
        tall = jnp.transpose(meta)[0:slot, :]
        columns_s.append((tall[:, 0:1] * COARSE + tall[:, 1:2]).astype(I32))
        columns_r.append((tall[:, 2:3] * COARSE + tall[:, 3:4]).astype(I32) - COARSE)
        rows_r.append((meta[2:3, 0:slot] * COARSE + meta[3:4, 0:slot]).astype(I32) - COARSE)
    column_s, column_r = jnp.concatenate(columns_s, axis=0), jnp.concatenate(columns_r, axis=0)
    receivers = mm(match_rows(column_r, span), table_ref[...]).astype(BF)
    edges = jnp.concatenate([ref[0:slot, :] for ref in slots], axis=0)
    product = mm(edges, win_ref[0:width, :])
    out_ref[...] = product + mm(receivers, win_ref[2 * width :, :])
    early_ref[...] = match_rows(column_s, 2 * span)
    late_ref[...] = match_rows(column_s, 2 * span, 2 * span)
    scatter_ref[...] = match_columns(jnp.concatenate(rows_r, axis=1), span)


def far_first_kernel(straight_ref, across_ref, pre_ref, early_ref, win_ref, out_ref):
    width = pre_ref.shape[1]
    table = jnp.concatenate([straight_ref[...], across_ref[...]], axis=0)
    senders = mm(early_ref[...], table).astype(BF)
    out_ref[...] = pre_ref[...] + mm(senders, win_ref[width : 2 * width, :])


def far_second_kernel(layer, lines, slot, start, chained, keep, *refs):
    straight_ref, across_ref, pre_ref, late_ref, scatter_ref, *refs = refs
    total, refs = (refs[0][...], refs[1:]) if chained else (None, refs)
    win_ref, wout_ref = refs[0:2]
    vecs, refs = [v[layer : layer + 1, :] for v in refs[2:5]], refs[5:]
    count = scatter_ref.shape[1] // slot
    slots, new_refs, sum_refs = refs[0:count], refs[count : 2 * count], refs[2 * count :]
    rows, width = slice(start * slot, (start + count) * slot), pre_ref.shape[1]
    table = jnp.concatenate([straight_ref[...], across_ref[...]], axis=0)
    senders = mm(late_ref[rows, :], table).astype(BF)
    pre_act = pre_ref[rows, :] + mm(senders, win_ref[width : 2 * width, :])
    normed = edge_tail(pre_act, wout_ref[...], *vecs)
    edges = jnp.concatenate([ref[0:slot, :] for ref in slots], axis=0)
    new = (edges.astype(F32) + normed).astype(BF)
    for j in range(count):
        new_refs[j][0:slot, :] = new[j * slot : (j + 1) * slot, :]
        if keep:
            new_refs[j][slot:, :] = slots[j][slot:, :]
    part = mm(scatter_ref[...], normed.astype(BF))
    total = part if total is None else total + part
    if len(sum_refs) == 1:
        sum_refs[0][...] = total
        return
    sum_refs[0][...] = total[0:COARSE, :]
    for i, ref in enumerate(sum_refs[1:]):
        ref[...] = total[(i + 1) * COARSE : (i + 2) * COARSE, :].astype(BF)


def node_tail(layer, nodes, pre_act, wout_ref, vec_refs):
    bias, gain, shift = [v[layer : layer + 1, :] for v in vec_refs]
    normed = edge_tail(pre_act, wout_ref[layer], bias, gain, shift)
    return (nodes.astype(F32) + normed).astype(BF)


def rest_kernel(layer, coarse_ref, nodes_ref, sum_ref, win_ref, wout_ref, *refs):
    nodes, width = nodes_ref[...], nodes_ref.shape[1]
    both = jnp.concatenate([coarse_ref[...], nodes], axis=0)
    pre_act = mm(both, win_ref[layer, 0:width, :])
    vec_refs, refs, coarse_pre_ref = refs[0:3], refs[3:-1], refs[-1]
    coarse_pre_ref[...] = pre_act[0:COARSE, :]
    sums = sum_ref[COARSE:, :].astype(BF)
    pre_act = pre_act[COARSE:, :] + mm(sums, win_ref[layer, width:, :])
    new = node_tail(layer, nodes, pre_act, wout_ref, vec_refs)
    if len(refs) == 1:
        refs[0][...] = new
        return
    pos_ref, *slot_refs, out_ref, half_ref, back_ref = refs
    out_ref[...] = new
    column, count = as_column(pos_ref[...]), back_ref.shape[1]
    slots = jnp.concatenate([ref[...] for ref in slot_refs], axis=0)
    half_ref[...] = mm(match_rows(column, count), slots).astype(BF)
    back_ref[...] = match_rows(column, count, count)


def coarse_kernel(layer, lines, nodes_ref, pre_ref, sum_ref, *refs):
    part_refs, refs = refs[0:lines], refs[lines:]
    (win_ref, wout_ref), vec_refs, refs = refs[0:2], refs[2:5], refs[5:]
    copies = []
    if len(refs) > 1:
        rest_ref, half_ref, back_ref, *slot_refs, out_hbm, far_hbm, out_ref, far_ref, sems = refs
        copies.append(pltpu.make_async_copy(rest_ref, out_hbm.at[COARSE:, :], sems.at[0]))
        copies[0].start()
        slots = jnp.concatenate([ref[...] for ref in slot_refs], axis=0)
        far_ref[...] = (half_ref[...].astype(F32) + mm(back_ref[...], slots)).astype(BF)
        copies.append(pltpu.make_async_copy(far_ref, far_hbm, sems.at[1]))
        copies[1].start()
    else:
        out_ref = refs[0]
    sums = sum_ref[0:COARSE, :] + part_refs[0][...]
    for ref in part_refs[1:]:
        sums = sums + ref[...].astype(F32)
    pre_act = pre_ref[...] + mm(sums.astype(BF), win_ref[layer, sums.shape[1] :, :])
    out_ref[...] = node_tail(layer, nodes_ref[...], pre_act, wout_ref, vec_refs)
    if copies:
        copies.append(pltpu.make_async_copy(out_ref, out_hbm.at[0:COARSE, :], sems.at[2]))
        copies[2].start()
        for copy in copies:
            copy.wait()


def call(kernel, outs, args, flops, limit, first=None, scratch=(), placed=pltpu.VMEM):
    bytes_accessed = sum(a.size * a.dtype.itemsize for a in [*args, *outs]) if flops or first == 0 else 0
    whole = pl.BlockSpec(memory_space=pltpu.VMEM)
    specs = [whole] * len(args)
    if first is not None:
        specs = [pl.BlockSpec(memory_space=pltpu.SMEM)] * first
        specs += [pl.BlockSpec(memory_space=pltpu.HBM)] * (len(args) - first)
        args = list(args[:first]) + [
            pltpu.with_memory_space_constraint(a, pltpu.HBM) for a in args[first:]
        ]
    return pl.pallas_call(
        kernel,
        out_shape=outs,
        in_specs=specs,
        out_specs=[pl.BlockSpec(memory_space=placed)] * len(outs),
        scratch_shapes=scratch,
        compiler_params=pltpu.CompilerParams(vmem_limit_bytes=limit),
        cost_estimate=pl.CostEstimate(flops=flops, bytes_accessed=bytes_accessed, transcendentals=0),
    )(*args)


def body(
    node_feat,
    local_edges,
    far_edges,
    local_send,
    local_recv,
    far_send,
    far_recv,
    edge_in,
    edge_out,
    node_in,
    node_out,
    edge_bias,
    edge_gain,
    edge_shift,
    node_bias,
    node_gain,
    node_shift,
):
    devices = lax.axis_size("patch")
    lines = devices // PLANE
    node_count, width = node_feat.shape
    far_count, local_count = far_edges.shape[0], local_edges.shape[0]
    slot = lines * (5 * far_count // (2 * devices))
    padded = -(-(slot + 4) // 16) * 16
    layers = edge_in.shape[0]
    limit = (24 if lines <= 4 else 56) * 2**20
    shape = jax.ShapeDtypeStruct

    def swap(values, distance):
        return lax.ppermute(values, "patch", [(i, i ^ distance) for i in range(devices)])

    own = lax.axis_index("patch").reshape(1).astype(I32)
    fs, fr = far_send.reshape(1, -1), far_recv.reshape(1, -1)
    tied = lax.optimization_barrier
    prepared = call(
        functools.partial(prep_kernel, node_count, lines, slot),
        [shape((1, far_count), I32), shape((COARSE, width), BF)]
        + [shape((node_count - COARSE, width), BF)]
        + [shape((padded, width), BF)] * PLANE,
        [own, fs, fr, far_edges, node_feat],
        2 * PLANE * slot * far_count * width,
        limit,
        first=1,
        scratch=[
            pltpu.VMEM((1, far_count), I32),
            pltpu.VMEM((1, far_count), I32),
            pltpu.VMEM((far_count, width), BF),
            pltpu.SemaphoreType.DMA((5,)),
        ],
    )
    pos, coarse, rest, slots = *prepared[0:3], prepared[3:]
    slots = [slots[0]] + [swap(slots[m], m) for m in range(1, PLANE)]
    def fetch(sources, picks):
        pieces = [sources[i] if layer is None else sources[i][0] for i, layer in picks]
        return call(
            functools.partial(load_kernel, picks),
            [shape(v.shape, v.dtype) for v in pieces],
            sources,
            0,
            limit,
            first=0,
            scratch=[pltpu.SemaphoreType.DMA((len(picks),))],
        )

    first = [local_edges, local_send, local_recv, edge_bias, edge_gain, edge_shift]
    picks = [(i, None) for i in range(len(first))] + [(len(first), 0), (len(first) + 1, 0)]
    first = fetch([*first, edge_in, edge_out], picks)
    far_rows, span = PLANE * slot, lines * COARSE
    cut = local_count // 3 * 2 // 256 * 256
    pieces = [slice(0, cut), slice(cut, local_count)] if cut else [slice(0, local_count)]
    local, local_send, local_recv = first[0:3]
    edge_vecs, weights = first[3:6], [first[6:8]]
    for l in range(layers):
        last = l == layers - 1

        def local_part(rows, before=(), share=1):
            return call(
                functools.partial(local_kernel, l, rows),
                [shape((rows.stop, width), BF), shape((node_count, width), F32)],
                [coarse, rest, local, local_send, local_recv, *weights[l], *edge_vecs, *before],
                2 * (rows.stop - rows.start) * width * (3 * node_count + 4 * width) * share,
                limit,
            )

        done = local_part(pieces[0], share=min(l, 1))
        if lines == 4:
            z2, z1 = swap(coarse, 8), swap(coarse, 4)
            if l:
                z2, z1, done = tied((z2, z1, done))
            else:
                z2, z1, done, slots = tied((z2, z1, done, slots))
            near = jnp.concatenate([coarse, z1, z2], axis=0)
            far_end = swap(z2, 4)
            across = swap(near, 2)
        else:
            near = [coarse] + [swap(coarse, PLANE * z) for z in range(1, lines)]
            near, far_end = jnp.concatenate(near[:-1], axis=0), near[-1]
            across = swap(near, 2)
        if not last:
            far_end, done = tied((far_end, done))
            for rows in pieces[1:]:
                done = local_part(rows, done)
        late = swap(far_end, 2)
        table = jnp.concatenate([near, far_end], axis=0)
        tables = [table, swap(table, 1)]
        pre_act, early, *found = call(
            functools.partial(far_ready_kernel, lines, slot),
            [shape((far_rows, width), F32)]
            + [shape((far_rows, 2 * span), BF)] * 2
            + [shape((span, far_rows), BF)],
            [*slots, table, weights[l][0]],
            2 * far_rows * width * (span + 2 * width),
            limit,
        )
        late, pre_act, found, done = tied((late, pre_act, found, done))
        late = jnp.concatenate([across, late], axis=0)
        late = [late, swap(late, 1)]
        pre_act = call(
            far_first_kernel,
            [shape((far_rows, width), F32)],
            [*tables, pre_act, early, weights[l][0]],
            2 * far_rows * width * (2 * span + width),
            limit,
        )
        found = [*pre_act, *found]
        moved = shape((slot if last else padded, width), BF)
        parts_shape = [shape((COARSE, width), F32)] + [shape((COARSE, width), BF)] * (lines - 1)

        def far_part(start, size, before, outs):
            return call(
                functools.partial(far_second_kernel, l, lines, slot, start, len(before) > 0, not last),
                [moved] * size + outs,
                [*late, *found[0:2], found[2 + start // size], *before]
                + [*weights[l], *edge_vecs, *slots[start : start + size]],
                2 * size * slot * width * (3 * span + 2 * width),
                limit,
            )

        far = far_part(0, PLANE, [], parts_shape)
        slots, parts = [*far[:PLANE]], far[PLANE:]
        if last:
            slots = [slots[0]] + [swap(slots[m], m) for m in range(1, PLANE)]
            parts, done = tied((parts, done))
            for rows in pieces[1:]:
                done = local_part(rows, done)
        local, sums = done
        far_parts = [swap(parts[z], PLANE * z) for z in [*range(2, lines), 1]]
        parts = [parts[0], *far_parts]
        if l == 0:
            sources = [node_in, node_out, node_bias, node_gain, node_shift]
            picks = [(i, None) for i in range(len(sources))]
            for i in range(1, layers):
                picks += [(len(sources), i), (len(sources) + 1, i)]
            sources, sums = tied(([*sources, edge_in, edge_out], sums))
            second = fetch(sources, picks)
            node_in, node_out, node_vecs = *second[0:2], second[2:5]
            weights += [second[5 + 2 * i : 7 + 2 * i] for i in range(layers - 1)]
        ends = [node_in, node_out, *node_vecs]
        *rest, coarse_pre = call(
            functools.partial(rest_kernel, l),
            [shape((node_count - COARSE, width), BF)]
            + [shape((far_count, width), BF), shape((far_count, 2 * slot), BF)] * last
            + [shape((COARSE, width), F32)],
            [coarse, rest, sums, *ends] + [pos, *slots[0:2]] * last,
            6 * (node_count - COARSE) * width * width,
            limit,
        )
        if last:
            return_shapes = [shape((node_count, width), BF), shape((far_count, width), BF)]
            extra = [*rest, *slots[2:]]
            scratch = [pltpu.VMEM((COARSE, width), BF), pltpu.VMEM((far_count, width), BF)]
            scratch += [pltpu.SemaphoreType.DMA((3,))]
        else:
            return_shapes, extra, rest = [shape((COARSE, width), BF)], [], rest[0]
        coarse, *far_out = call(
            functools.partial(coarse_kernel, l, lines),
            return_shapes,
            [coarse, coarse_pre, sums, *parts, *ends, *extra],
            6 * COARSE * width * width,
            limit,
            scratch=scratch if last else (),
            placed=pltpu.HBM if last else pltpu.VMEM,
        )
    return (coarse, local, far_out[0])


def solution(mesh):
    split = P(("groups", "patch"), None)
    line = P(("groups", "patch"))
    return jax.shard_map(
        body,
        mesh=mesh,
        in_specs=(split,) * 3 + (line,) * 4 + (P(),) * 10,
        out_specs=(split,) * 3,
        check_vma=False,
    )
```
